32 devices in a mesh: dp: 8 (over z, core), ctx: 4 (over y, x).
Axes of the slice: x: 2, y: 2, z: 4, core: 2. Of those that a mesh axis runs over, the one named last changes fastest.
Arguments:
- layer_input: bfloat16 [8192, 1536], P(('dp', 'ctx')), may hold values from -6 to 6
- cotangent: bfloat16 [8192, 1536], P(('dp', 'ctx')), may hold values from -6 to 6
- doc_lengths: int32 [8, 5], P('dp'), may hold values from 1 to 512, 1024 in all within a row
- attention_gain: bfloat16 [1536], P(('dp', 'ctx')), may hold values from 0.5 to 1.5
- query_weight: bfloat16 [1536, 1536], P(('dp', 'ctx')), may hold values from -0.15625 to 0.15625
- key_weight: bfloat16 [1536, 256], P(('dp', 'ctx')), may hold values from -0.15625 to 0.15625
- value_weight: bfloat16 [1536, 256], P(('dp', 'ctx')), may hold values from -0.15625 to 0.15625
- query_bias: bfloat16 [1536], P(('dp', 'ctx')), may hold values from -3 to 3
- key_bias: bfloat16 [256], P(('dp', 'ctx')), may hold values from -3 to 3
- value_bias: bfloat16 [256], P(('dp', 'ctx')), may hold values from -3 to 3
- output_weight: bfloat16 [1536, 1536], P(('dp', 'ctx')), may hold values from -0.625 to 0.625
- feedforward_gain: bfloat16 [1536], P(('dp', 'ctx')), may hold values from 0.5 to 1.5
- gate_weight: bfloat16 [1536, 8960], P(('dp', 'ctx')), may hold values from -0.15625 to 0.15625
- up_weight: bfloat16 [1536, 8960], P(('dp', 'ctx')), may hold values from -0.15625 to 0.15625
- down_weight: bfloat16 [8960, 1536], P(('dp', 'ctx')), may hold values from -0.0625 to 0.0625
Outputs:
- layer_output: bfloat16 [8192, 1536], P(('dp', 'ctx'))
- input_grad: float32 [8192, 1536], P(('dp', 'ctx'))
- attention_gain_grad: float32 [1536], P(('dp', 'ctx'))
- query_weight_grad: float32 [1536, 1536], P(('dp', 'ctx'))
- key_weight_grad: float32 [1536, 256], P(('dp', 'ctx'))
- value_weight_grad: float32 [1536, 256], P(('dp', 'ctx'))
- query_bias_grad: float32 [1536], P(('dp', 'ctx'))
- key_bias_grad: float32 [256], P(('dp', 'ctx'))
- value_bias_grad: float32 [256], P(('dp', 'ctx'))
- output_weight_grad: float32 [1536, 1536], P(('dp', 'ctx'))
- feedforward_gain_grad: float32 [1536], P(('dp', 'ctx'))
- gate_weight_grad: float32 [1536, 8960], P(('dp', 'ctx'))
- up_weight_grad: float32 [1536, 8960], P(('dp', 'ctx'))
- down_weight_grad: float32 [8960, 1536], P(('dp', 'ctx'))
The draws below stay inside these ranges and needn't reach their ends.
Inputs may be any that keep to these rules, and one draw needn't show every extreme that they name: `doc_lengths`: each row sums to 1024; its last entry counts padding tokens at the row's end; each row's largest entry is exactly 512.
All inputs are finite; a program needn't handle non-finite values.
Results may differ from the reference program's by a relative error of at most 0.024.
Values may be sent and summed in bfloat16 or wider, within the bound.
No kernel may reach another device: no remote copies, remote signals or barrier semaphores. Data moves between devices by JAX's collectives and lax.ppermute only.
A program may use at most 384 MiB of HBM per device.

```python
import math
import jax
import jax.numpy as jnp
import numpy as np
from jax import lax

D = 1536
HEADS = 12
KV_HEADS = 2
HEAD = 128
FF = 8960
ROW = 1024
DOCS = 5
MOST = 512
TOKENS = 8192
N_DP = 8


def level_of(own_key, dims, shards, least, high):
    def one(axis_at, shards_of):
        steps = jax.random.uniform(jax.random.fold_in(jax.random.fold_in(own_key, 6), axis_at), (shards_of,), jnp.float32, least / len(shards), high / len(shards))
        return jnp.repeat(jnp.exp(steps), dims[axis_at] // shards_of).reshape((-1,) + (1,) * (len(dims) - axis_at - 1))

    gain = one(*shards[0])
    for cut in shards[1:]:
        gain = gain * one(*cut)
    return gain


def profile(amount, total, bound, slope):
    portions = [(1 << 20) // math.isqrt(rank ** slope) + 1 for rank in range(2, amount + 1)]
    spare, holding = total - bound - (amount - 1), [1] * (amount - 1)
    while spare > 0:
        movable = [i for i in range(amount - 1) if holding[i] < bound]
        whole, budget = sum([portions[i] for i in movable]), spare
        for i in movable:
            addition = min(bound - holding[i], max(1, budget * portions[i] // whole), spare)
            holding[i] = holding[i] + addition
            spare = spare - addition
    return np.array([bound] + holding)


def ragged_sizes(rng, amount, total, most, slope):
    if amount == 2:
        one = jax.random.randint(rng, (), max(1, total - most), min(most, total - 1) + 1)
        return jnp.stack([one, total - one])
    sizes = jnp.asarray(profile(amount, total, most, slope), jnp.int32)
    twos = (amount - 1) // 2
    donor, taker = sizes[1:1 + 2 * twos:2], sizes[2:2 + 2 * twos:2]
    slack = jnp.minimum(donor - 1, most - taker)
    passed = jax.random.randint(jax.random.fold_in(rng, 1), (twos,), 0, 1 << 20) % (slack + 1)
    sizes = sizes.at[1:1 + 2 * twos:2].set(donor - passed).at[2:2 + 2 * twos:2].set(taker + passed)
    return sizes[jax.random.permutation(jax.random.fold_in(rng, 2), amount)]


def scatter_about(rng, dims, scale, reach, cuts=(), kind=jnp.bfloat16):
    factor_of = level_of(rng, dims, cuts, -0.22, 0.18) if cuts else 1.0
    array = jax.random.normal(rng, dims, jnp.float32) * scale * factor_of
    return jnp.minimum(jnp.maximum(array, -reach), reach).astype(kind)


def setup_inputs(seed: int = 0) -> dict:
    seeds = jax.random.split(jax.random.key(seed), 16)
    layer_input = scatter_about(seeds[0], (TOKENS, D), 1.0, 6.0, ((0, 32),))
    cotangent = scatter_about(seeds[1], (TOKENS, D), 1.0, 6.0, ((0, 32),))
    doc_lengths = jax.vmap(lambda own: ragged_sizes(own, DOCS, ROW, MOST, 2))(jax.random.split(seeds[2], N_DP)).reshape((N_DP, DOCS)).astype(jnp.int32)
    attention_gain = jnp.clip(1.0 + 0.1 * jax.random.normal(seeds[3], (D,), jnp.float32), 0.5, 1.5).astype(jnp.bfloat16)
    query_weight = scatter_about(seeds[4], (D, D), D ** -0.5, 0.15625, ((0, 32),))
    key_weight = scatter_about(seeds[5], (D, KV_HEADS * HEAD), D ** -0.5, 0.15625, ((0, 32),))
    value_weight = scatter_about(seeds[6], (D, KV_HEADS * HEAD), D ** -0.5, 0.15625, ((0, 32),))
    query_bias = scatter_about(seeds[7], (D,), 0.5, 3.0, ((0, 32),))
    key_bias = scatter_about(seeds[8], (KV_HEADS * HEAD,), 0.5, 3.0, ((0, 32),))
    value_bias = scatter_about(seeds[9], (KV_HEADS * HEAD,), 0.5, 3.0, ((0, 32),))
    output_weight = scatter_about(seeds[10], (D, D), (D // 16) ** -0.5, 0.625, ((0, 32),))
    feedforward_gain = jnp.clip(1.0 + 0.1 * jax.random.normal(seeds[11], (D,), jnp.float32), 0.5, 1.5).astype(jnp.bfloat16)
    gate_weight = scatter_about(seeds[12], (D, FF), D ** -0.5, 0.15625, ((0, 32),))
    up_weight = scatter_about(seeds[13], (D, FF), D ** -0.5, 0.15625, ((0, 32),))
    down_weight = scatter_about(seeds[14], (FF, D), FF ** -0.5, 0.0625, ((0, 32),))
    return dict(layer_input=layer_input, cotangent=cotangent, doc_lengths=doc_lengths, attention_gain=attention_gain, query_weight=query_weight, key_weight=key_weight, value_weight=value_weight, query_bias=query_bias, key_bias=key_bias, value_bias=value_bias, output_weight=output_weight, feedforward_gain=feedforward_gain, gate_weight=gate_weight, up_weight=up_weight, down_weight=down_weight)


EPS = 1e-06
HIGHEST = lax.Precision.HIGHEST

@jax.custom_vjp
def low(v):
    return lax.optimization_barrier(v.astype(jnp.bfloat16)).astype(jnp.float32)

@jax.custom_vjp
def low_back(v):
    return v

def low_keep(v):
    return (low(v), None)

def low_pass(kept, grad):
    return (grad,)

def back_keep(v):
    return (v, None)

def back_low(kept, grad):
    return (low(grad),)
low.defvjp(low_keep, low_pass)
low_back.defvjp(back_keep, back_low)

def layout(lengths):
    places = jnp.arange(ROW, dtype=jnp.int32)
    ends = jnp.cumsum(lengths).astype(jnp.int32)
    starts = ends - lengths
    segment = lax.optimization_barrier(jnp.sum((places[:, None] >= ends[None, :]).astype(jnp.int32), axis=1))
    chosen = (segment[:, None] == jnp.arange(DOCS, dtype=jnp.int32)[None, :]).astype(jnp.int32)
    offsets = places - lax.optimization_barrier(jnp.sum(chosen * starts[None, :], axis=1))
    padded = segment == DOCS - 1
    allowed = (places[None, :] <= places[:, None]) & (segment[None, :] == segment[:, None])
    allowed = allowed & (jnp.logical_not(padded)[None, :] | (places[None, :] == places[:, None]))
    freqs = 10000.0 ** (-jnp.arange(0, HEAD // 2, dtype=jnp.float32) * 2.0 / HEAD)
    angles = offsets.astype(jnp.float32)[:, None] * freqs[None, :]
    return (jnp.cos(angles), jnp.sin(angles), allowed)

def turn(values, cosine, sine):
    half = values.shape[-1] // 2
    first = values[..., :half]
    second = values[..., half:]
    cosine = cosine[:, None, :]
    sine = sine[:, None, :]
    return jnp.concatenate([first * cosine - second * sine, second * cosine + first * sine], axis=-1)

def matmul(left, right):
    return jnp.dot(left, right, precision=HIGHEST, preferred_element_type=jnp.float32)

def forward(params, hidden, cosine, sine, allowed):
    gain_a, weight_q, weight_k, weight_v, bias_q, bias_k, bias_v, weight_o, gain_f, weight_g, weight_u, weight_d = params
    inverse = lax.rsqrt(lax.optimization_barrier(jnp.mean(hidden * hidden, axis=1, keepdims=True)) + EPS)
    normed = low(hidden * inverse * gain_a)
    queries = matmul(normed, weight_q) + bias_q
    keys = matmul(normed, weight_k) + bias_k
    values = matmul(normed, weight_v) + bias_v
    queries = low(turn(low_back(queries).reshape(ROW, HEADS, HEAD), cosine, sine))
    keys = low(turn(low_back(keys).reshape(ROW, KV_HEADS, HEAD), cosine, sine))
    values = low(low_back(values)).reshape(ROW, KV_HEADS, HEAD)
    grouped = queries.reshape(ROW, KV_HEADS, HEADS // KV_HEADS, HEAD)
    scores = jnp.einsum('tkgd,skd->kgts', grouped, keys, precision=HIGHEST) * HEAD ** (-0.5)
    scores = low_back(scores)
    scores = jnp.where(allowed[None, None], scores, -1e+30)
    top = lax.optimization_barrier(jnp.max(scores, axis=-1, keepdims=True))
    weights = jnp.exp(scores - top)
    probs = weights / lax.optimization_barrier(jnp.sum(weights, axis=-1, keepdims=True))
    mixed = jnp.einsum('kgts,skd->tkgd', low(probs), values, precision=HIGHEST).reshape(ROW, D)
    mixed = low(low_back(mixed))
    middle = hidden + low_back(matmul(mixed, weight_o))
    inverse2 = lax.rsqrt(lax.optimization_barrier(jnp.mean(middle * middle, axis=1, keepdims=True)) + EPS)
    normed2 = low(middle * inverse2 * gain_f)
    gate = low_back(matmul(normed2, weight_g))
    upward = low_back(matmul(normed2, weight_u))
    active = low(gate * jax.nn.sigmoid(gate) * upward)
    return middle + matmul(active, weight_d)

def reference(layer_input, cotangent, doc_lengths, attention_gain, query_weight, key_weight, value_weight, query_bias, key_bias, value_bias, output_weight, feedforward_gain, gate_weight, up_weight, down_weight):
    params = tuple((param.astype(jnp.float32) for param in (attention_gain, query_weight, key_weight, value_weight, query_bias, key_bias, value_bias, output_weight, feedforward_gain, gate_weight, up_weight, down_weight)))
    hidden_rows = layer_input.astype(jnp.float32).reshape(N_DP, ROW, D)
    cotangent_rows = cotangent.astype(jnp.float32).reshape(N_DP, ROW, D)

    def one_row(totals, inputs):
        hidden, upstream, lengths = inputs
        cosine, sine, allowed = layout(lengths)

        def run(params_in, hidden_in):
            return forward(params_in, hidden_in, cosine, sine, allowed)
        result, pullback = jax.vjp(run, params, hidden)
        grads, hidden_grad = pullback(upstream)
        totals = jax.tree.map(lambda left, right: left + right, totals, grads)
        return (totals, (result.astype(jnp.bfloat16), hidden_grad))
    zeros = tuple((jnp.zeros(param.shape, jnp.float32) for param in params))
    totals, (results, hidden_grads) = lax.scan(one_row, zeros, (hidden_rows, cotangent_rows, doc_lengths))
    return (results.reshape(N_DP * ROW, D), hidden_grads.reshape(N_DP * ROW, D), totals[0], totals[1], totals[2], totals[3], totals[4], totals[5], totals[6], totals[7], totals[8], totals[9], totals[10], totals[11])
```

```python
import jax
import jax.numpy as jnp
from jax import lax
from jax.sharding import PartitionSpec as P

D = 1536
HEADS = 12
KV_HEADS = 2
HEAD = 128
DOCS = 5


EPS = 1e-06
F32 = jnp.float32
LOW = jnp.bfloat16


def turn(values, cosine, sine):
    half = values.shape[-1] // 2
    first = values[..., :half]
    second = values[..., half:]
    cosine = cosine[:, None, :]
    sine = sine[:, None, :]
    return jnp.concatenate(
        [first * cosine - second * sine, second * cosine + first * sine], axis=-1
    )


def unturn(grads, cosine, sine):
    half = grads.shape[-1] // 2
    first = grads[..., :half]
    second = grads[..., half:]
    cosine = cosine[:, None, :]
    sine = sine[:, None, :]
    return jnp.concatenate(
        [first * cosine + second * sine, second * cosine - first * sine], axis=-1
    )


def score_block(query_rot, key_all, allowed):
    tokens = query_rot.shape[0]
    grouped = query_rot.reshape(tokens, KV_HEADS, HEADS // KV_HEADS, HEAD)
    keyed = key_all.reshape(key_all.shape[0], KV_HEADS, HEAD)
    scores = jnp.einsum(
        "tkgd,skd->kgts", grouped, keyed, preferred_element_type=F32
    ) * HEAD ** (-0.5)
    return jnp.where(allowed[None, None], scores, -1e30)


def norm_back(grad_normed, hidden, inverse, gain):
    scaled = grad_normed * gain
    grad_gain = jnp.sum(grad_normed * hidden * inverse, axis=0)
    grad_hidden = inverse * scaled - hidden * inverse**3 * jnp.mean(
        scaled * hidden, axis=1, keepdims=True
    )
    return (grad_gain, grad_hidden)


class Line:
    def __init__(self, axis, size, stride):
        self.axis, self.size, self.stride = axis, size, stride
        total = lax.axis_size(axis)
        self.place = (lax.axis_index(axis) // stride) % size
        self.up = []
        for i in range(total):
            place = (i // stride) % size
            self.up.append((i, i + ((place + 1) % size - place) * stride))

    def shift(self, value):
        return lax.ppermute(value, self.axis, self.up)

    def ring(self, value):
        parts = [value]
        for _ in range(self.size - 1):
            parts.append(self.shift(parts[-1]))
        return parts

    def ordered(self, parts, dim):
        if self.size == 2:
            first = self.place == 0
            return jnp.stack(
                [jnp.where(first, parts[0], parts[1]), jnp.where(first, parts[1], parts[0])], dim
            )
        shape = parts[0].shape
        whole = jnp.zeros(shape[:dim] + (self.size,) + shape[dim:], parts[0].dtype)
        for step, part in enumerate(parts):
            whole = lax.dynamic_update_slice_in_dim(
                whole, jnp.expand_dims(part, dim), (self.place - step) % self.size, dim
            )
        return whole

    def gather(self, value, dim):
        return self.ordered(self.ring(value), dim)

    def pick(self, blocks, dim, step):
        return lax.dynamic_index_in_dim(blocks, (self.place - step) % self.size, dim, False)

    def scatter(self, blocks, dim, kind=LOW):
        total = self.pick(blocks, dim, 1)
        for step in range(2, self.size + 1):
            total = self.shift(total.astype(kind)).astype(F32)
            total = total + self.pick(blocks, dim, step).astype(F32)
        return total


def per_device(
    layer_input,
    cotangent,
    doc_lengths,
    attention_gain,
    query_weight,
    key_weight,
    value_weight,
    query_bias,
    key_bias,
    value_bias,
    output_weight,
    feedforward_gain,
    gate_weight,
    up_weight,
    down_weight,
):
    tokens = layer_input.shape[0]
    n_dp = lax.axis_size("dp")
    n_ctx = lax.axis_size("ctx")
    here = lax.axis_index("dp")
    which = lax.axis_index("ctx")
    chip = Line("dp", n_dp // 2, 2)
    core = Line("dp", 2, 1)
    outer = Line("ctx", n_ctx // 2, 2)
    inner = Line("ctx", 2, 1)
    rows = query_weight.shape[0]
    kv_width = KV_HEADS * HEAD

    def plane_gather(value, first, dim):
        if first:
            return outer.gather(inner.gather(value, dim), dim)
        return inner.gather(outer.gather(value, dim), dim + 1)

    def plane_scatter(blocks, first, dim, kind=LOW):
        if first:
            return outer.scatter(inner.scatter(blocks, dim + 1, kind), dim, kind)
        return inner.scatter(outer.scatter(blocks, dim, kind), dim, kind)

    def all_gather(value, first):
        gathered = plane_gather(chip.gather(value, 0), first, 1)
        return core.gather(gathered, 1)

    def all_scatter(blocks, first, kind=LOW):
        return chip.scatter(
            plane_scatter(core.scatter(blocks, 1, kind), first, 1, kind), 0, kind
        )

    def split_owners(array):
        return array.reshape((n_dp // 2, 2, n_ctx // 2, 2, -1) + array.shape[1:])

    vectors = jnp.concatenate(
        [attention_gain, feedforward_gain, query_bias, key_bias, value_bias]
    )[None]
    vectors = all_gather(vectors, True).reshape(n_dp * n_ctx, -1)
    cuts = [rows, 2 * rows, 3 * rows, 3 * rows + key_bias.shape[0]]
    gain_a, gain_f, bias_q, bias_k, bias_v = (
        part.reshape(-1).astype(F32) for part in jnp.split(vectors, cuts, axis=1)
    )
    mixed_weight = jnp.concatenate([query_weight, key_weight, value_weight], axis=1)
    half = mixed_weight.shape[1] // 2
    weight_in = [
        all_gather(mixed_weight[:, :half], True).reshape(D, half),
        all_gather(mixed_weight[:, half:], False).reshape(D, half),
    ]
    weight_o = jnp.concatenate(
        [
            all_gather(output_weight[:, : D // 2], True).reshape(D, D // 2),
            all_gather(output_weight[:, D // 2 :], False).reshape(D, D // 2),
        ],
        axis=1,
    )

    width = gate_weight.shape[1] // n_dp
    units = jnp.stack(
        [gate_weight.reshape(rows, n_dp, width), up_weight.reshape(rows, n_dp, width)]
    ).transpose(2, 0, 1, 3)

    def exchange(blocks):
        got = jnp.zeros(blocks.shape, blocks.dtype)
        own = lax.dynamic_index_in_dim(blocks, here, 0, True)
        got = lax.dynamic_update_slice_in_dim(got, own, here, 0)
        for step in range(1, n_dp):
            there = lax.dynamic_index_in_dim(blocks, (here + step) % n_dp, 0, True)
            arrived = lax.ppermute(there, "dp", [(i, (i + step) % n_dp) for i in range(n_dp)])
            got = lax.dynamic_update_slice_in_dim(got, arrived, (here - step) % n_dp, 0)
        return got

    units = exchange(units)
    weight_g = plane_gather(units[:, 0], True, 1).reshape(D, width)
    weight_u = plane_gather(units[:, 1], False, 1).reshape(D, width)
    weight_d = jnp.concatenate(
        [
            plane_gather(down_weight[:, : D // 2], True, 0).reshape(width, D // 2),
            plane_gather(down_weight[:, D // 2 :], False, 0).reshape(width, D // 2),
        ],
        axis=1,
    )

    def token_chunks(value):
        return [
            jnp.concatenate([part, core.shift(part)], axis=0) for part in chip.ring(value)
        ]

    upstream = token_chunks(cotangent)

    whole = tokens * n_ctx
    places = jnp.arange(whole, dtype=jnp.int32)
    lengths = doc_lengths[0]
    order = jnp.arange(DOCS, dtype=jnp.int32)
    ends = jnp.sum(jnp.where(order[None, :] <= order[:, None], lengths[None, :], 0), axis=1)
    starts = ends - lengths
    segment = jnp.sum((places[:, None] >= ends[None, :]).astype(jnp.int32), axis=1)
    chosen = (segment[:, None] == order[None, :]).astype(jnp.int32)
    offsets = places - jnp.sum(chosen * starts[None, :], axis=1)
    padded = segment == DOCS - 1
    first_row = which * tokens
    mine = lax.dynamic_slice_in_dim(places, first_row, tokens)
    my_segment = lax.dynamic_slice_in_dim(segment, first_row, tokens)
    my_offsets = lax.dynamic_slice_in_dim(offsets, first_row, tokens)
    allowed = (places[None, :] <= mine[:, None]) & (segment[None, :] == my_segment[:, None])
    allowed = allowed & (jnp.logical_not(padded)[None, :] | (places[None, :] == mine[:, None]))
    freqs = 10000.0 ** (-jnp.arange(0, HEAD // 2, dtype=F32) * 2.0 / HEAD)
    angles = my_offsets.astype(F32)[:, None] * freqs[None, :]
    cosine = jnp.cos(angles)
    sine = jnp.sin(angles)

    hidden = layer_input.astype(F32)
    inverse = lax.rsqrt(jnp.mean(hidden * hidden, axis=1, keepdims=True) + EPS)
    normed = (hidden * inverse * gain_a).astype(LOW)
    projected = jnp.concatenate(
        [jnp.dot(normed, part, preferred_element_type=F32) for part in weight_in], axis=1
    )
    queries = projected[:, :D] + bias_q
    keys = projected[:, D : D + kv_width] + bias_k
    values = projected[:, D + kv_width :] + bias_v
    query_rot = turn(queries.reshape(tokens, HEADS, HEAD), cosine, sine).astype(LOW)
    key_rot = (
        turn(keys.reshape(tokens, KV_HEADS, HEAD), cosine, sine)
        .astype(LOW)
        .reshape(tokens, kv_width)
    )
    value_low = values.astype(LOW)
    key_all = plane_gather(key_rot, True, 0).reshape(whole, kv_width)
    value_all = plane_gather(value_low, False, 0).reshape(whole, kv_width)
    scores = score_block(query_rot, key_all, allowed)
    top = jnp.max(scores, axis=-1, keepdims=True)
    weights = jnp.exp(scores - top)
    totals = jnp.sum(weights, axis=-1, keepdims=True)
    probs = weights / totals
    log_total = top + jnp.log(totals)
    value_heads = value_all.reshape(whole, KV_HEADS, HEAD)
    mixed = jnp.einsum(
        "kgts,skd->tkgd", probs.astype(LOW), value_heads, preferred_element_type=F32
    )
    mixed_low = mixed.reshape(tokens, D).astype(LOW)
    middle = hidden + jnp.dot(mixed_low, weight_o, preferred_element_type=F32)

    inverse2 = lax.rsqrt(jnp.mean(middle * middle, axis=1, keepdims=True) + EPS)
    normed2 = (middle * inverse2 * gain_f).astype(LOW)
    inputs = token_chunks(normed2)
    actives, grad_gates, grad_upwards, outs, grads = [], [], [], [], []
    for fed, back in zip(inputs, upstream):
        gate = jnp.dot(fed, weight_g, preferred_element_type=F32)
        upward = jnp.dot(fed, weight_u, preferred_element_type=F32)
        grad_active = jnp.einsum("td,fd->tf", back, weight_d, preferred_element_type=F32)
        sigmoid_gate = jax.nn.sigmoid(gate)
        active = (gate * sigmoid_gate * upward).astype(LOW)
        grad_gate = (
            grad_active * upward * sigmoid_gate * (1.0 + gate * (1.0 - sigmoid_gate))
        ).astype(LOW)
        grad_upward = (grad_active * gate * sigmoid_gate).astype(LOW)
        grads.append(
            jnp.einsum("tf,df->td", grad_gate, weight_g, preferred_element_type=F32)
            + jnp.einsum("tf,df->td", grad_upward, weight_u, preferred_element_type=F32)
        )
        outs.append(jnp.dot(active, weight_d, preferred_element_type=F32))
        actives.append(active)
        grad_gates.append(grad_gate)
        grad_upwards.append(grad_upward)

    def token_sums(parts):
        kept = [part[:tokens] + core.shift(part[tokens:].astype(LOW)).astype(F32) for part in parts]
        total = kept[1 % len(kept)]
        for step in range(2, len(kept) + 1):
            total = chip.shift(total.astype(LOW)).astype(F32) + kept[step % len(kept)]
        return total

    grad_normed2 = token_sums(grads)
    layer_output = (middle + token_sums(outs)).astype(LOW)

    fed_all = jnp.concatenate(inputs, axis=0)
    back_all = jnp.concatenate(upstream, axis=0)
    part_gate = jnp.einsum(
        "td,tf->df", fed_all, jnp.concatenate(grad_gates, axis=0), preferred_element_type=F32
    ).astype(LOW)
    part_up = jnp.einsum(
        "td,tf->df", fed_all, jnp.concatenate(grad_upwards, axis=0), preferred_element_type=F32
    ).astype(LOW)
    part_down = jnp.einsum(
        "tf,td->fd", jnp.concatenate(actives, axis=0), back_all, preferred_element_type=F32
    ).astype(LOW)

    def by_plane(part):
        return part.reshape((n_dp, n_ctx // 2, 2, rows) + part.shape[1:])

    sum_gate = plane_scatter(by_plane(part_gate), True, 1).astype(LOW)
    sum_up = plane_scatter(by_plane(part_up), False, 1).astype(LOW)
    sums = exchange(jnp.stack([sum_gate, sum_up], axis=1))
    gate_weight_grad = sums[:, 0].transpose(1, 0, 2).reshape(rows, -1).astype(F32)
    up_weight_grad = sums[:, 1].transpose(1, 0, 2).reshape(rows, -1).astype(F32)
    down_parts = part_down.reshape(n_ctx // 2, 2, width // n_ctx, D)
    down_weight_grad = jnp.concatenate(
        [
            plane_scatter(down_parts[..., : D // 2], True, 0),
            plane_scatter(down_parts[..., D // 2 :], False, 0),
        ],
        axis=1,
    )

    grad_gain_f, grad_middle = norm_back(grad_normed2, middle, inverse2, gain_f)
    grad_middle = grad_middle + cotangent.astype(F32)
    grad_attention = grad_middle.astype(LOW)
    part_output = jnp.einsum(
        "td,te->de", mixed_low, grad_attention, preferred_element_type=F32
    ).astype(LOW)
    part_output = split_owners(part_output)
    output_weight_grad = jnp.concatenate(
        [
            all_scatter(part_output[..., : D // 2], True),
            all_scatter(part_output[..., D // 2 :], False),
        ],
        axis=1,
    )
    grad_mixed = jnp.einsum(
        "te,de->td", grad_attention, weight_o, preferred_element_type=F32
    ).astype(LOW)
    grad_heads = grad_mixed.reshape(tokens, KV_HEADS, HEADS // KV_HEADS, HEAD)
    probs = jnp.exp(score_block(query_rot, key_all, allowed) - log_total)
    grad_probs = jnp.einsum(
        "tkgd,skd->kgts", grad_heads, value_heads, preferred_element_type=F32
    )
    grad_scores = (
        probs * (grad_probs - jnp.sum(probs * grad_probs, axis=-1, keepdims=True))
    ).astype(LOW)
    grad_value_part = jnp.einsum(
        "kgts,tkgd->skd", probs.astype(LOW), grad_heads, preferred_element_type=F32
    )
    key_heads = key_all.reshape(whole, KV_HEADS, HEAD)
    grouped = query_rot.reshape(tokens, KV_HEADS, HEADS // KV_HEADS, HEAD)
    grad_query_rot = jnp.einsum(
        "kgts,skd->tkgd", grad_scores, key_heads, preferred_element_type=F32
    ) * HEAD ** (-0.5)
    grad_key_part = jnp.einsum(
        "kgts,tkgd->skd", grad_scores, grouped, preferred_element_type=F32
    ) * HEAD ** (-0.5)
    plane_shape = (n_ctx // 2, 2, tokens, kv_width)
    grad_key_rot = plane_scatter(grad_key_part.reshape(plane_shape), True, 0)
    grad_values = plane_scatter(grad_value_part.reshape(plane_shape), False, 0).astype(LOW)
    grad_keys = (
        unturn(grad_key_rot.reshape(tokens, KV_HEADS, HEAD), cosine, sine)
        .reshape(tokens, kv_width)
        .astype(LOW)
    )
    grad_queries = (
        unturn(grad_query_rot.reshape(tokens, HEADS, HEAD), cosine, sine)
        .reshape(tokens, D)
        .astype(LOW)
    )
    joined = jnp.concatenate([grad_queries, grad_keys, grad_values], axis=1)
    parts_in = [joined[:, :half], joined[:, half:]]
    scattered = [
        all_scatter(
            split_owners(
                jnp.einsum("td,te->de", normed, part, preferred_element_type=F32).astype(LOW)
            ),
            first,
        )
        for part, first in zip(parts_in, (True, False))
    ]
    in_grads = jnp.concatenate(scattered, axis=1)
    grad_normed = sum(
        jnp.einsum("te,de->td", part, weight, preferred_element_type=F32)
        for part, weight in zip(parts_in, weight_in)
    )
    grad_gain_a, grad_hidden = norm_back(grad_normed, hidden, inverse, gain_a)
    input_grad = grad_middle + grad_hidden
    bias_sums = jnp.sum(joined.astype(F32), axis=0)
    owners = n_dp * n_ctx
    small = jnp.concatenate(
        [
            part.reshape(owners, -1)
            for part in (
                grad_gain_a,
                grad_gain_f,
                bias_sums[:D],
                bias_sums[D : D + kv_width],
                bias_sums[D + kv_width :],
            )
        ],
        axis=1,
    )
    small = all_scatter(split_owners(small), True, F32)
    small_gain_a, small_gain_f, small_q, small_k, small_v = jnp.split(small[0], cuts)
    return (
        layer_output,
        input_grad,
        small_gain_a,
        in_grads[:, :D],
        in_grads[:, D : D + kv_width],
        in_grads[:, D + kv_width :],
        small_q,
        small_k,
        small_v,
        output_weight_grad,
        small_gain_f,
        gate_weight_grad,
        up_weight_grad,
        down_weight_grad,
    )


def solution(mesh):
    split = P(("dp", "ctx"), None)
    vector = P(("dp", "ctx"))
    placed = (
        split,
        split,
        P("dp", None),
        vector,
        split,
        split,
        split,
        vector,
        vector,
        vector,
        split,
        vector,
        split,
        split,
        split,
    )
    results = (
        split,
        split,
        vector,
        split,
        split,
        split,
        vector,
        vector,
        vector,
        split,
        vector,
        split,
        split,
        split,
    )
    return jax.shard_map(
        per_device, mesh=mesh, in_specs=placed, out_specs=results, check_vma=False
    )
```

```python
import jax
import jax.numpy as jnp
from jax import lax
from jax.sharding import PartitionSpec as P

D = 1536
HEADS = 12
KV_HEADS = 2
HEAD = 128
DOCS = 5


EPS = 1e-06
F32 = jnp.float32
LOW = jnp.bfloat16


def turn(values, cosine, sine):
    half = values.shape[-1] // 2
    first = values[..., :half]
    second = values[..., half:]
    cosine = cosine[:, None, :]
    sine = sine[:, None, :]
    return jnp.concatenate(
        [first * cosine - second * sine, second * cosine + first * sine], axis=-1
    )


def unturn(grads, cosine, sine):
    half = grads.shape[-1] // 2
    first = grads[..., :half]
    second = grads[..., half:]
    cosine = cosine[:, None, :]
    sine = sine[:, None, :]
    return jnp.concatenate(
        [first * cosine + second * sine, second * cosine - first * sine], axis=-1
    )


def score_block(query_rot, key_all, allowed):
    tokens = query_rot.shape[0]
    grouped = query_rot.reshape(tokens, KV_HEADS, HEADS // KV_HEADS, HEAD)
    keyed = key_all.reshape(key_all.shape[0], KV_HEADS, HEAD)
    scores = jnp.einsum(
        "tkgd,skd->kgts", grouped, keyed, preferred_element_type=F32
    ) * HEAD ** (-0.5)
    return jnp.where(allowed[None, None], scores, -1e30)


def norm_back(grad_normed, hidden, inverse, gain):
    scaled = grad_normed * gain
    grad_gain = jnp.sum(grad_normed * hidden * inverse, axis=0)
    grad_hidden = inverse * scaled - hidden * inverse**3 * jnp.mean(
        scaled * hidden, axis=1, keepdims=True
    )
    return (grad_gain, grad_hidden)


def hold(value, *others):
    for other in others:
        first = other[(0,) * other.ndim]
        value = jnp.where(first != first, jnp.zeros_like(value), value)
    return value


class Line:
    def __init__(self, axis, size, stride):
        self.axis, self.size, self.stride = axis, size, stride
        total = lax.axis_size(axis)
        self.place = (lax.axis_index(axis) // stride) % size
        self.up = []
        for i in range(total):
            place = (i // stride) % size
            self.up.append((i, i + ((place + 1) % size - place) * stride))

    def shift(self, value):
        return lax.ppermute(value, self.axis, self.up)

    def ring(self, value):
        parts = [value]
        for _ in range(self.size - 1):
            parts.append(self.shift(parts[-1]))
        return parts

    def ordered(self, parts, dim):
        if self.size == 2:
            first = self.place == 0
            return jnp.stack(
                [jnp.where(first, parts[0], parts[1]), jnp.where(first, parts[1], parts[0])], dim
            )
        shape = parts[0].shape
        whole = jnp.zeros(shape[:dim] + (self.size,) + shape[dim:], parts[0].dtype)
        for step, part in enumerate(parts):
            whole = lax.dynamic_update_slice_in_dim(
                whole, jnp.expand_dims(part, dim), (self.place - step) % self.size, dim
            )
        return whole

    def gather(self, value, dim):
        return self.ordered(self.ring(value), dim)

    def direct(self, blocks, dim, *waits):
        total = self.pick(blocks, dim, 0).astype(F32)
        sent = [hold(self.pick(blocks, dim, -step), *waits) for step in range(1, self.size)]
        for step, block in enumerate(sent, 1):
            total = total + lax.ppermute(
                block, self.axis, [(i, self.there(i, step)) for i in range(len(self.up))]
            ).astype(F32)
        return total

    def there(self, i, step):
        place = (i // self.stride) % self.size
        return i + ((place + step) % self.size - place) * self.stride

    def pick(self, blocks, dim, step):
        return lax.dynamic_index_in_dim(blocks, (self.place - step) % self.size, dim, False)

    def scatter(self, blocks, dim, kind=LOW):
        total = self.pick(blocks, dim, 1)
        for step in range(2, self.size + 1):
            total = self.shift(total.astype(kind)).astype(F32)
            total = total + self.pick(blocks, dim, step).astype(F32)
        return total


def per_device(
    layer_input,
    cotangent,
    doc_lengths,
    attention_gain,
    query_weight,
    key_weight,
    value_weight,
    query_bias,
    key_bias,
    value_bias,
    output_weight,
    feedforward_gain,
    gate_weight,
    up_weight,
    down_weight,
):
    tokens = layer_input.shape[0]
    n_dp = lax.axis_size("dp")
    n_ctx = lax.axis_size("ctx")
    here = lax.axis_index("dp")
    which = lax.axis_index("ctx")
    chip = Line("dp", n_dp // 2, 2)
    core = Line("dp", 2, 1)
    outer = Line("ctx", n_ctx // 2, 2)
    inner = Line("ctx", 2, 1)
    row = Line("ctx", n_ctx, 1)
    rows = query_weight.shape[0]
    kv_width = KV_HEADS * HEAD

    def plane_gather(value, first, dim):
        if first:
            return outer.gather(inner.gather(value, dim), dim)
        return inner.gather(outer.gather(value, dim), dim + 1)

    def plane_scatter(blocks, first, dim, kind=LOW):
        if first:
            return outer.scatter(inner.scatter(blocks, dim + 1, kind), dim, kind)
        return inner.scatter(outer.scatter(blocks, dim, kind), dim, kind)

    def plane_gather_halves(value, cut, dim):
        return (
            plane_gather(value[..., :cut], True, dim),
            plane_gather(value[..., cut:], False, dim),
        )

    def plane_sums(array, cut, *waits):
        blocks = array.reshape((n_dp // 2, 2, n_ctx // 2, 2, rows) + array.shape[1:])
        blocks = hold(core.scatter(blocks, 1).astype(LOW), *waits)
        return [
            plane_scatter(part, first, 1).astype(LOW)
            for part, first in ((blocks[..., :cut], True), (blocks[..., cut:], False))
        ]

    few = key_bias.shape[0]
    tile = jnp.stack(
        [attention_gain, feedforward_gain, query_bias]
        + [jnp.pad(part, (0, rows - few)) for part in (key_bias, value_bias)],
        axis=1,
    )
    tile = jnp.pad(tile, ((0, 0), (0, HEAD - tile.shape[1])))
    mixed_width = D + 2 * kv_width
    half = D + kv_width
    ring_in = chip.ring(
        jnp.concatenate([query_weight, key_weight, value_weight, output_weight, tile], axis=1)
    )
    plane_in = plane_gather_halves(chip.ordered(ring_in, 0), half, 1)
    weight_qk, weight_rest = [core.gather(part, 1).reshape(D, -1) for part in plane_in]
    weight_v = weight_rest[:, :kv_width]
    weight_o = weight_rest[:, kv_width : kv_width + D]
    vectors = weight_rest[:, kv_width + D :].astype(F32).T
    gain_a, gain_f, bias_q = vectors[0], vectors[1], vectors[2]
    bias_k, bias_v = (
        vectors[i].reshape(-1, rows)[:, :few].reshape(-1) for i in (3, 4)
    )

    real = gate_weight.shape[1] // n_dp
    width = -(-real // HEAD) * HEAD
    weight_d = jnp.concatenate(
        [part.reshape(real, D // 2) for part in plane_gather_halves(down_weight, D // 2, 0)],
        axis=1,
    )
    weight_d = jnp.pad(weight_d, ((0, width - real), (0, 0)))
    units = jnp.stack(
        [gate_weight.reshape(rows, n_dp, real), up_weight.reshape(rows, n_dp, real)]
    ).transpose(2, 0, 1, 3)
    units = jnp.pad(units, ((0, 0), (0, 0), (0, 0), (0, width - real)))
    units = lax.all_to_all(hold(units, ring_in[-1]), "dp", 0, 0, tiled=True)
    units = units.transpose(1, 0, 2, 3).reshape(2 * n_dp * rows, width)
    units_all = lax.all_gather(hold(units, weight_qk), "ctx", axis=0, tiled=True)
    units_all = units_all.reshape(n_ctx, 2, n_dp * rows, width)
    weight_g, weight_u = (units_all[:, i].reshape(D, width) for i in (0, 1))
    place = jnp.arange(D, dtype=jnp.int32)
    source = ((place // rows) % n_dp * n_ctx + place // (rows * n_dp)) * rows + place % rows
    order = (place[:, None] == source[None, :]).astype(LOW)

    upstream_all = lax.all_gather(hold(cotangent, ring_in[-1]), "dp", axis=0, tiled=True)

    whole = tokens * n_ctx
    places = jnp.arange(whole, dtype=jnp.int32)
    lengths = doc_lengths[0]
    entry = jnp.arange(DOCS, dtype=jnp.int32)
    ends = jnp.sum(jnp.where(entry[None, :] <= entry[:, None], lengths[None, :], 0), axis=1)
    starts = ends - lengths
    segment = jnp.sum((places[:, None] >= ends[None, :]).astype(jnp.int32), axis=1)
    chosen = (segment[:, None] == entry[None, :]).astype(jnp.int32)
    offsets = places - jnp.sum(chosen * starts[None, :], axis=1)
    padded = segment == DOCS - 1
    first_row = which * tokens
    mine = lax.dynamic_slice_in_dim(places, first_row, tokens)
    my_segment = lax.dynamic_slice_in_dim(segment, first_row, tokens)
    my_offsets = lax.dynamic_slice_in_dim(offsets, first_row, tokens)
    allowed = (places[None, :] <= mine[:, None]) & (segment[None, :] == my_segment[:, None])
    allowed = allowed & (jnp.logical_not(padded)[None, :] | (places[None, :] == mine[:, None]))
    freqs = 10000.0 ** (-jnp.arange(0, HEAD // 2, dtype=F32) * 2.0 / HEAD)
    angles = my_offsets.astype(F32)[:, None] * freqs[None, :]
    cosine = jnp.cos(angles)
    sine = jnp.sin(angles)

    hidden = layer_input.astype(F32)
    inverse = lax.rsqrt(jnp.mean(hidden * hidden, axis=1, keepdims=True) + EPS)
    normed = (hidden * inverse * gain_a).astype(LOW)
    projected = jnp.dot(normed, weight_qk, preferred_element_type=F32)
    queries = projected[:, :D] + bias_q
    keys = projected[:, D:] + bias_k
    values = jnp.dot(normed, weight_v, preferred_element_type=F32) + bias_v
    query_rot = turn(queries.reshape(tokens, HEADS, HEAD), cosine, sine).astype(LOW)
    key_rot = (
        turn(keys.reshape(tokens, KV_HEADS, HEAD), cosine, sine)
        .astype(LOW)
        .reshape(tokens, kv_width)
    )
    value_low = values.astype(LOW)
    both = jnp.concatenate([key_rot, value_low], axis=1)
    both_all = jnp.zeros((n_ctx,) + both.shape, LOW)
    for step in range(n_ctx):
        arrived = both
        if step:
            arrived = lax.ppermute(both, "ctx", [(i, (i + step) % n_ctx) for i in range(n_ctx)])
        both_all = lax.dynamic_update_slice_in_dim(
            both_all, arrived[None], (which - step) % n_ctx, 0
        )
    both_all = both_all.reshape(whole, 2 * kv_width)
    key_all, value_all = both_all[:, :kv_width], both_all[:, kv_width:]
    scores = score_block(query_rot, key_all, allowed)
    top = jnp.max(scores, axis=-1, keepdims=True)
    weights = jnp.exp(scores - top)
    totals = jnp.sum(weights, axis=-1, keepdims=True)
    probs = weights / totals
    log_total = top + jnp.log(totals)
    value_heads = value_all.reshape(whole, KV_HEADS, HEAD)
    mixed = jnp.einsum(
        "kgts,skd->tkgd", probs.astype(LOW), value_heads, preferred_element_type=F32
    )
    mixed_low = mixed.reshape(tokens, D).astype(LOW)
    middle = hidden + jnp.dot(mixed_low, weight_o, preferred_element_type=F32)

    inverse2 = lax.rsqrt(jnp.mean(middle * middle, axis=1, keepdims=True) + EPS)
    normed2 = (middle * inverse2 * gain_f).astype(LOW)
    normed2 = jnp.dot(normed2, order, preferred_element_type=F32).astype(LOW)
    upstream_own = [
        lax.dynamic_slice_in_dim(
            upstream_all, ((chip.place - step) % chip.size * 2 + core.place) * tokens, tokens, 0
        )
        for step in range(n_dp // 2)
    ]
    upstream_other = [
        lax.dynamic_slice_in_dim(
            upstream_all, ((chip.place - step) % chip.size * 2 + 1 - core.place) * tokens, tokens, 0
        )
        for step in range(n_dp // 2)
    ]
    upstream = [
        jnp.concatenate([own, other], axis=0) for own, other in zip(upstream_own, upstream_other)
    ]
    grad_actives = [
        jnp.einsum("td,fd->tf", back, weight_d, preferred_element_type=F32).astype(LOW)
        for back in upstream
    ]
    normed2 = hold(normed2, weight_g, weight_u, *grad_actives[:1])
    inputs_own = chip.ring(normed2)

    def both_cores(part, *waits):
        part = hold(part, *waits)
        return jnp.concatenate([part, core.shift(part)], axis=0)

    def core_sum(part):
        return part[:tokens] + core.shift(part[tokens:].astype(LOW)).astype(F32)

    inputs, actives, grad_gates, grad_upwards, grads, kept, grad_sums, outs = ([] for _ in range(8))
    out_all = jnp.zeros((n_dp * tokens, D), LOW)
    for step, fed in enumerate(inputs_own):
        fed = both_cores(fed, *actives[-1:])
        inputs.append(fed)
        grad_active = grad_actives[step].astype(F32)
        if step > 1:
            fed = hold(fed, *kept, *grad_sums[1:], *outs[-1:])
        gate = jnp.dot(fed, weight_g, preferred_element_type=F32)
        upward = jnp.dot(fed, weight_u, preferred_element_type=F32)
        sigmoid_gate = jax.nn.sigmoid(gate)
        active = (gate * sigmoid_gate * upward).astype(LOW)
        grad_gate = (
            grad_active * upward * sigmoid_gate * (1.0 + gate * (1.0 - sigmoid_gate))
        ).astype(LOW)
        grad_upward = (grad_active * gate * sigmoid_gate).astype(LOW)
        grads.append(
            jnp.einsum("tf,df->td", grad_gate, weight_g, preferred_element_type=F32)
            + jnp.einsum("tf,df->td", grad_upward, weight_u, preferred_element_type=F32)
        )
        kept.append(core_sum(grads[-1]))
        if step == 1:
            grad_sums.append(kept[1])
        if step > 1:
            arrived = chip.shift(grad_sums[-1].astype(LOW)).astype(F32)
            grad_sums.append(arrived + kept[step])
        actives.append(active)
        outs.append(jnp.dot(active, weight_d, preferred_element_type=F32).astype(LOW))
        for side in range(2):
            index = (chip.place - step) % chip.size * 2 + (core.place + side) % 2
            piece = outs[-1][side * tokens : (side + 1) * tokens]
            out_all = lax.dynamic_update_slice_in_dim(out_all, piece, index * tokens, 0)
        grad_gates.append(grad_gate)
        grad_upwards.append(grad_upward)
    arrived = chip.shift(grad_sums[-1].astype(LOW)).astype(F32)
    grad_normed2 = (arrived + kept[0]).astype(LOW)

    fed_all = jnp.concatenate(inputs, axis=0)
    part_gate = jnp.einsum(
        "td,tf->df",
        fed_all,
        hold(jnp.concatenate(grad_gates, axis=0), grad_sums[-1]),
        preferred_element_type=F32,
    ).astype(LOW)
    def plane_sum(part):
        total = lax.psum_scatter(part, "ctx", scatter_dimension=0, tiled=True)
        return total.reshape(n_dp, rows, width)


    grad_normed2 = hold(grad_normed2, part_gate)
    grad_normed2 = jnp.einsum("te,de->td", grad_normed2, order, preferred_element_type=F32)
    grad_gain_f, grad_middle = norm_back(grad_normed2, middle, inverse2, gain_f)
    grad_middle = grad_middle + cotangent.astype(F32)
    grad_attention = grad_middle.astype(LOW)
    part_up = jnp.einsum(
        "td,tf->df",
        fed_all,
        hold(jnp.concatenate(grad_upwards, axis=0), grad_attention),
        preferred_element_type=F32,
    ).astype(LOW)
    sums = jnp.stack([plane_sum(part_gate), plane_sum(part_up)], axis=1)
    part_output = jnp.einsum(
        "td,te->de", mixed_low, grad_attention, preferred_element_type=F32
    ).astype(LOW)
    grad_mixed = jnp.einsum(
        "te,de->td", grad_attention, weight_o, preferred_element_type=F32
    ).astype(LOW)
    grad_heads = grad_mixed.reshape(tokens, KV_HEADS, HEADS // KV_HEADS, HEAD)
    probs = jnp.exp(score_block(query_rot, key_all, allowed) - log_total)
    grad_probs = jnp.einsum(
        "tkgd,skd->kgts", grad_heads, value_heads, preferred_element_type=F32
    )
    grad_scores = (
        probs * (grad_probs - jnp.sum(probs * grad_probs, axis=-1, keepdims=True))
    ).astype(LOW)
    grad_value_part = jnp.einsum(
        "kgts,tkgd->skd", probs.astype(LOW), grad_heads, preferred_element_type=F32
    )
    key_heads = key_all.reshape(whole, KV_HEADS, HEAD)
    grouped = query_rot.reshape(tokens, KV_HEADS, HEADS // KV_HEADS, HEAD)
    grad_query_rot = jnp.einsum(
        "kgts,skd->tkgd", grad_scores, key_heads, preferred_element_type=F32
    ) * HEAD ** (-0.5)
    grad_key_part = jnp.einsum(
        "kgts,tkgd->skd", grad_scores, grouped, preferred_element_type=F32
    ) * HEAD ** (-0.5)
    both_part = jnp.concatenate(
        [grad_key_part.reshape(whole, kv_width), grad_value_part.reshape(whole, kv_width)], axis=1
    )
    both_part = both_part.astype(LOW).reshape(n_ctx, tokens, 2 * kv_width)
    both_sum = row.direct(both_part, 0)
    grad_key_rot = both_sum[:, :kv_width]
    grad_values = both_sum[:, kv_width:].astype(LOW)
    part_out = lax.psum_scatter(out_all, "dp", scatter_dimension=0, tiled=True)
    sums = lax.all_to_all(hold(sums, both_part), "dp", 0, 0, tiled=True)
    gate_weight_grad = sums[:, 0, :, :real].transpose(1, 0, 2).reshape(rows, -1).astype(F32)
    up_weight_grad = sums[:, 1, :, :real].transpose(1, 0, 2).reshape(rows, -1).astype(F32)
    plane_output = plane_sums(part_output, D // 2, grad_key_rot)
    grad_keys = (
        unturn(grad_key_rot.reshape(tokens, KV_HEADS, HEAD), cosine, sine)
        .reshape(tokens, kv_width)
        .astype(LOW)
    )
    grad_queries = (
        unturn(grad_query_rot.reshape(tokens, HEADS, HEAD), cosine, sine)
        .reshape(tokens, D)
        .astype(LOW)
    )
    joined = jnp.concatenate([grad_queries, grad_keys, grad_values], axis=1)
    grad_normed = jnp.einsum(
        "te,de->td", joined[:, :half], weight_qk, preferred_element_type=F32
    ) + jnp.einsum("te,de->td", grad_values, weight_v, preferred_element_type=F32)
    grad_gain_a, grad_hidden = norm_back(grad_normed, hidden, inverse, gain_a)
    input_grad = grad_middle + grad_hidden
    part_in = jnp.einsum("td,te->de", normed, joined, preferred_element_type=F32).astype(LOW)
    bias_sums = jnp.sum(joined.astype(F32), axis=0)
    short = [
        jnp.pad(part.reshape(-1, few), ((0, 0), (0, rows - few))).reshape(D)
        for part in (bias_sums[D : D + kv_width], bias_sums[D + kv_width :])
    ]
    tile = jnp.stack([grad_gain_a, grad_gain_f, bias_sums[:D]] + short, axis=1).astype(LOW)
    tile = jnp.pad(tile, ((0, 0), (0, HEAD - tile.shape[1])))
    part_in = jnp.concatenate([part_in, tile], axis=1)
    part_down = jnp.einsum(
        "tf,td->fd",
        hold(jnp.concatenate(actives, axis=0), part_in),
        jnp.concatenate(upstream, axis=0),
        preferred_element_type=F32,
    ).astype(LOW)[:real]
    part_down = lax.psum_scatter(part_down, "ctx", scatter_dimension=0, tiled=True)
    plane_grads = plane_sums(part_in, mixed_width // 2, sums)
    plane_grads = jnp.concatenate(plane_grads + plane_output, axis=-1)
    layer_output = (middle + hold(part_out, plane_grads).astype(F32)).astype(LOW)
    down_weight_grad = hold(part_down, plane_grads).astype(F32)
    in_grads = chip.scatter(plane_grads, 0)
    output_weight_grad = in_grads[:, mixed_width + HEAD :]
    small = in_grads[:, mixed_width : mixed_width + HEAD].T
    return (
        layer_output,
        input_grad,
        small[0],
        in_grads[:, :D],
        in_grads[:, D : D + kv_width],
        in_grads[:, D + kv_width : mixed_width],
        small[2],
        small[3, :few],
        small[4, :few],
        output_weight_grad,
        small[1],
        gate_weight_grad,
        up_weight_grad,
        down_weight_grad,
    )


def solution(mesh):
    split = P(("dp", "ctx"), None)
    vector = P(("dp", "ctx"))
    placed = (
        split,
        split,
        P("dp", None),
        vector,
        split,
        split,
        split,
        vector,
        vector,
        vector,
        split,
        vector,
        split,
        split,
        split,
    )
    results = (
        split,
        split,
        vector,
        split,
        split,
        split,
        vector,
        vector,
        vector,
        split,
        vector,
        split,
        split,
        split,
    )
    return jax.shard_map(
        per_device, mesh=mesh, in_specs=placed, out_specs=results, check_vma=False
    )
```

```python
import jax
import jax.numpy as jnp
from jax import lax
from jax.experimental import pallas as pl
from jax.experimental.pallas import tpu as pltpu
from jax.sharding import PartitionSpec as P

D = 1536
HEADS = 12
KV_HEADS = 2
HEAD = 128
DOCS = 5


EPS = 1e-06
F32 = jnp.float32
LOW = jnp.bfloat16
GROUP = HEADS // KV_HEADS
VMEM_BYTES = 32 * 2**20
LAST = (((1,), (1,)), ((), ()))
FIRST = (((0,), (0,)), ((), ()))


def turn(values, cosine, sine):
    half = values.shape[-1] // 2
    first = values[..., :half]
    second = values[..., half:]
    cosine = cosine[:, None, :]
    sine = sine[:, None, :]
    return jnp.concatenate(
        [first * cosine - second * sine, second * cosine + first * sine], axis=-1
    )


def unturn(grads, cosine, sine):
    half = grads.shape[-1] // 2
    first = grads[..., :half]
    second = grads[..., half:]
    cosine = cosine[:, None, :]
    sine = sine[:, None, :]
    return jnp.concatenate(
        [first * cosine + second * sine, second * cosine - first * sine], axis=-1
    )


def product(left, right, contract):
    return lax.dot_general(left, right, contract, preferred_element_type=F32)


def attend_kernel(q_ref, k_ref, v_ref, bias_ref, o_ref):
    scores = product(q_ref[...], k_ref[...], LAST) * HEAD ** (-0.5) + bias_ref[...]
    weights = jnp.exp(scores - jnp.max(scores, axis=1, keepdims=True))
    probs = weights * (1.0 / jnp.sum(weights, axis=1, keepdims=True))
    o_ref[...] = jnp.dot(probs.astype(LOW), v_ref[...], preferred_element_type=F32).astype(LOW)


def attend(query_rot, both_all, bias):
    tokens, whole = bias.shape
    return pl.pallas_call(
        attend_kernel,
        grid=(HEADS,),
        in_specs=[
            pl.BlockSpec((tokens, HEAD), lambda h: (0, h)),
            pl.BlockSpec((whole, HEAD), lambda h: (0, h // GROUP)),
            pl.BlockSpec((whole, HEAD), lambda h: (0, KV_HEADS + h // GROUP)),
            pl.BlockSpec((tokens, whole), lambda h: (0, 0)),
        ],
        out_specs=pl.BlockSpec((tokens, HEAD), lambda h: (0, h)),
        out_shape=jax.ShapeDtypeStruct(query_rot.shape, LOW),
        compiler_params=pltpu.CompilerParams(vmem_limit_bytes=VMEM_BYTES),
        cost_estimate=pl.CostEstimate(flops=10**10, bytes_accessed=10**6, transcendentals=0),
    )(query_rot, both_all, both_all, bias)


def attend_back_kernel(q_ref, g_ref, k_ref, v_ref, bias_ref, dq_ref, dkv_ref, dk_sum, dv_sum):
    step = pl.program_id(0) % GROUP
    query, grad, key = q_ref[...], g_ref[...], k_ref[...]
    scores = product(key, query, LAST) * HEAD ** (-0.5) + bias_ref[...]
    weights = jnp.exp(scores - jnp.max(scores, axis=0, keepdims=True))
    probs = weights * (1.0 / jnp.sum(weights, axis=0, keepdims=True))
    grad_probs = product(v_ref[...], grad, LAST)
    mean = jnp.sum(probs * grad_probs, axis=0, keepdims=True)
    grad_scores = (probs * (grad_probs - mean)).astype(LOW)
    dq_ref[...] = product(grad_scores, key, FIRST) * HEAD ** (-0.5)
    dv = jnp.dot(probs.astype(LOW), grad, preferred_element_type=F32)
    dk = jnp.dot(grad_scores, query, preferred_element_type=F32)

    @pl.when(step == 0)
    def _():
        dv_sum[...] = dv
        dk_sum[...] = dk

    @pl.when(step > 0)
    def _():
        dv_sum[...] += dv
        dk_sum[...] += dk

    @pl.when(step == GROUP - 1)
    def _():
        dkv_ref[0] = (dk_sum[...] * HEAD ** (-0.5)).astype(LOW)
        dkv_ref[1] = dv_sum[...].astype(LOW)


def attend_back(query_rot, grad_mixed, both_all, bias):
    whole, tokens = bias.shape
    return pl.pallas_call(
        attend_back_kernel,
        grid=(HEADS,),
        in_specs=[
            pl.BlockSpec((tokens, HEAD), lambda h: (0, h)),
            pl.BlockSpec((tokens, HEAD), lambda h: (0, h)),
            pl.BlockSpec((whole, HEAD), lambda h: (0, h // GROUP)),
            pl.BlockSpec((whole, HEAD), lambda h: (0, KV_HEADS + h // GROUP)),
            pl.BlockSpec((whole, tokens), lambda h: (0, 0)),
        ],
        out_specs=[
            pl.BlockSpec((tokens, HEAD), lambda h: (0, h)),
            pl.BlockSpec((2, whole, HEAD), lambda h: (0, 0, h // GROUP)),
        ],
        out_shape=[
            jax.ShapeDtypeStruct(query_rot.shape, F32),
            jax.ShapeDtypeStruct((2, whole, KV_HEADS * HEAD), LOW),
        ],
        scratch_shapes=[pltpu.VMEM((whole, HEAD), F32), pltpu.VMEM((whole, HEAD), F32)],
        compiler_params=pltpu.CompilerParams(vmem_limit_bytes=VMEM_BYTES),
        cost_estimate=pl.CostEstimate(flops=2 * 10**10, bytes_accessed=10**6, transcendentals=0),
    )(query_rot, grad_mixed, both_all, both_all, bias)


def norm_back(grad_normed, hidden, inverse, gain):
    scaled = grad_normed * gain
    grad_gain = jnp.sum(grad_normed * hidden * inverse, axis=0)
    grad_hidden = inverse * scaled - hidden * inverse**3 * jnp.mean(
        scaled * hidden, axis=1, keepdims=True
    )
    return (grad_gain, grad_hidden)


def hold(value, *others):
    for other in others:
        first = other[(0,) * other.ndim]
        value = jnp.where(first != first, jnp.zeros_like(value), value)
    return value


class Line:
    def __init__(self, axis, size, stride):
        self.axis, self.size, self.stride = axis, size, stride
        total = lax.axis_size(axis)
        self.place = (lax.axis_index(axis) // stride) % size
        self.up = []
        for i in range(total):
            place = (i // stride) % size
            self.up.append((i, i + ((place + 1) % size - place) * stride))

    def shift(self, value):
        return lax.ppermute(value, self.axis, self.up)

    def ring(self, value):
        parts = [value]
        for _ in range(self.size - 1):
            parts.append(self.shift(parts[-1]))
        return parts

    def ordered(self, parts, dim):
        if self.size == 2:
            first = self.place == 0
            return jnp.stack(
                [jnp.where(first, parts[0], parts[1]), jnp.where(first, parts[1], parts[0])], dim
            )
        shape = parts[0].shape
        whole = jnp.zeros(shape[:dim] + (self.size,) + shape[dim:], parts[0].dtype)
        for step, part in enumerate(parts):
            whole = lax.dynamic_update_slice_in_dim(
                whole, jnp.expand_dims(part, dim), (self.place - step) % self.size, dim
            )
        return whole

    def gather(self, value, dim):
        return self.ordered(self.ring(value), dim)

    def direct(self, blocks, dim, *waits):
        total = self.pick(blocks, dim, 0).astype(F32)
        sent = [hold(self.pick(blocks, dim, -step), *waits) for step in range(1, self.size)]
        for step, block in enumerate(sent, 1):
            total = total + lax.ppermute(
                block, self.axis, [(i, self.there(i, step)) for i in range(len(self.up))]
            ).astype(F32)
        return total

    def there(self, i, step):
        place = (i // self.stride) % self.size
        return i + ((place + step) % self.size - place) * self.stride

    def pick(self, blocks, dim, step):
        return lax.dynamic_index_in_dim(blocks, (self.place - step) % self.size, dim, False)

    def scatter(self, blocks, dim, kind=LOW):
        total = self.pick(blocks, dim, 1)
        for step in range(2, self.size + 1):
            total = self.shift(total.astype(kind)).astype(F32)
            total = total + self.pick(blocks, dim, step).astype(F32)
        return total


def per_device(
    layer_input,
    cotangent,
    doc_lengths,
    attention_gain,
    query_weight,
    key_weight,
    value_weight,
    query_bias,
    key_bias,
    value_bias,
    output_weight,
    feedforward_gain,
    gate_weight,
    up_weight,
    down_weight,
):
    tokens = layer_input.shape[0]
    n_dp = lax.axis_size("dp")
    n_ctx = lax.axis_size("ctx")
    here = lax.axis_index("dp")
    which = lax.axis_index("ctx")
    chip = Line("dp", n_dp // 2, 2)
    core = Line("dp", 2, 1)
    outer = Line("ctx", n_ctx // 2, 2)
    inner = Line("ctx", 2, 1)
    row = Line("ctx", n_ctx, 1)
    rows = query_weight.shape[0]
    kv_width = KV_HEADS * HEAD

    def plane_gather(value, first, dim):
        if first:
            return outer.gather(inner.gather(value, dim), dim)
        return inner.gather(outer.gather(value, dim), dim + 1)

    def plane_scatter(blocks, first, dim, kind=LOW):
        if first:
            return outer.scatter(inner.scatter(blocks, dim + 1, kind), dim, kind)
        return inner.scatter(outer.scatter(blocks, dim, kind), dim, kind)

    def plane_gather_halves(value, cut, dim):
        first = (inner.gather(value[..., :cut], dim), outer.gather(value[..., cut:], dim))
        first = (hold(first[0], first[1]), hold(first[1], first[0]))
        return (outer.gather(first[0], dim), inner.gather(first[1], dim + 1))

    def core_sums(array):
        blocks = array.reshape((n_dp // 2, 2, n_ctx // 2, 2, rows) + array.shape[1:])
        return core.scatter(blocks, 1).astype(LOW)

    few = key_bias.shape[0]
    tile = jnp.stack(
        [attention_gain, feedforward_gain, query_bias]
        + [jnp.pad(part, (0, rows - few)) for part in (key_bias, value_bias)],
        axis=1,
    )
    tile = jnp.pad(tile, ((0, 0), (0, HEAD - tile.shape[1])))
    mixed_width = D + 2 * kv_width
    half = D + kv_width
    ring_in = chip.ring(
        jnp.concatenate([query_weight, key_weight, value_weight, output_weight, tile], axis=1)
    )
    cut = D // 2
    down_first = (inner.gather(down_weight[:, :cut], 0), outer.gather(down_weight[:, cut:], 0))
    plane_in = plane_gather_halves(hold(chip.ordered(ring_in, 0), *down_first), half, 1)
    upstream_all = lax.all_gather(hold(cotangent, ring_in[-1]), "dp", axis=0, tiled=True)

    real = gate_weight.shape[1] // n_dp
    width = -(-real // HEAD) * HEAD
    units = jnp.stack(
        [gate_weight.reshape(rows, n_dp, real), up_weight.reshape(rows, n_dp, real)]
    ).transpose(2, 0, 1, 3)
    units = jnp.pad(units, ((0, 0), (0, 0), (0, 0), (0, width - real)))
    units = lax.all_to_all(hold(units, *plane_in), "dp", 0, 0, tiled=True)
    weight_qk, weight_rest = [core.gather(hold(part, *plane_in), 1).reshape(D, -1) for part in plane_in]
    weight_v = weight_rest[:, :kv_width]
    weight_o = weight_rest[:, kv_width : kv_width + D]
    vectors = weight_rest[:, kv_width + D :].astype(F32).T
    gain_a, gain_f, bias_q = vectors[0], vectors[1], vectors[2]
    bias_k, bias_v = (
        vectors[i].reshape(-1, rows)[:, :few].reshape(-1) for i in (3, 4)
    )

    place = jnp.arange(D, dtype=jnp.int32)
    source = ((place // rows) % n_dp * n_ctx + place // (rows * n_dp)) * rows + place % rows
    order = (place[:, None] == source[None, :]).astype(LOW)

    whole = tokens * n_ctx
    places = jnp.arange(whole, dtype=jnp.int32)
    lengths = doc_lengths[0]
    entry = jnp.arange(DOCS, dtype=jnp.int32)
    ends = jnp.sum(jnp.where(entry[None, :] <= entry[:, None], lengths[None, :], 0), axis=1)
    starts = ends - lengths
    segment = jnp.sum((places[:, None] >= ends[None, :]).astype(jnp.int32), axis=1)
    chosen = (segment[:, None] == entry[None, :]).astype(jnp.int32)
    offsets = places - jnp.sum(chosen * starts[None, :], axis=1)
    padded = segment == DOCS - 1
    first_row = which * tokens
    mine = lax.dynamic_slice_in_dim(places, first_row, tokens)
    my_segment = lax.dynamic_slice_in_dim(segment, first_row, tokens)
    my_offsets = lax.dynamic_slice_in_dim(offsets, first_row, tokens)
    allowed = (places[None, :] <= mine[:, None]) & (segment[None, :] == my_segment[:, None])
    allowed = allowed & (jnp.logical_not(padded)[None, :] | (places[None, :] == mine[:, None]))
    bias = jnp.where(allowed, 0.0, -1e30).astype(F32)
    turned = (places[:, None] <= mine[None, :]) & (segment[:, None] == my_segment[None, :])
    turned = turned & (jnp.logical_not(padded)[:, None] | (places[:, None] == mine[None, :]))
    bias_turned = jnp.where(turned, 0.0, -1e30).astype(F32)
    freqs = 10000.0 ** (-jnp.arange(0, HEAD // 2, dtype=F32) * 2.0 / HEAD)
    angles = my_offsets.astype(F32)[:, None] * freqs[None, :]
    cosine = jnp.cos(angles)
    sine = jnp.sin(angles)

    hidden = layer_input.astype(F32)
    inverse = lax.rsqrt(jnp.mean(hidden * hidden, axis=1, keepdims=True) + EPS)
    normed = (hidden * inverse * gain_a).astype(LOW)
    projected = jnp.dot(normed, weight_qk, preferred_element_type=F32)
    queries = projected[:, :D] + bias_q
    keys = projected[:, D:] + bias_k
    values = jnp.dot(normed, weight_v, preferred_element_type=F32) + bias_v
    query_rot = turn(queries.reshape(tokens, HEADS, HEAD), cosine, sine).astype(LOW)
    key_rot = (
        turn(keys.reshape(tokens, KV_HEADS, HEAD), cosine, sine)
        .astype(LOW)
        .reshape(tokens, kv_width)
    )
    value_low = values.astype(LOW)
    down_parts = (
        outer.gather(hold(down_first[0], weight_qk), 0),
        inner.gather(hold(down_first[1], weight_qk), 1),
    )
    weight_d = jnp.concatenate([part.reshape(real, cut) for part in down_parts], axis=1)
    weight_d = jnp.pad(weight_d, ((0, width - real), (0, 0)))
    both = hold(jnp.concatenate([key_rot, value_low], axis=1), *down_parts)
    both_all = jnp.zeros((n_ctx,) + both.shape, LOW)
    for step in range(n_ctx):
        arrived = both
        if step:
            arrived = lax.ppermute(both, "ctx", [(i, (i + step) % n_ctx) for i in range(n_ctx)])
        both_all = lax.dynamic_update_slice_in_dim(
            both_all, arrived[None], (which - step) % n_ctx, 0
        )
    both_all = both_all.reshape(whole, 2 * kv_width)
    units = units.transpose(1, 0, 2, 3).reshape(2 * n_dp * rows, width)
    units_all = lax.all_gather(hold(units, both), "ctx", axis=0, tiled=True)
    units_all = units_all.reshape(n_ctx, 2, n_dp * rows, width)
    weight_g, weight_u = (units_all[:, i].reshape(D, width) for i in (0, 1))
    mixed_low = attend(query_rot.reshape(tokens, D), both_all, bias)
    middle = hidden + jnp.dot(mixed_low, weight_o, preferred_element_type=F32)

    inverse2 = lax.rsqrt(jnp.mean(middle * middle, axis=1, keepdims=True) + EPS)
    normed2 = (middle * inverse2 * gain_f).astype(LOW)
    normed2 = jnp.dot(normed2, order, preferred_element_type=F32).astype(LOW)
    upstream = [
        lax.dynamic_slice_in_dim(
            upstream_all, (chip.place - step) % chip.size * 2 * tokens, 2 * tokens, 0
        )
        for step in range(n_dp // 2)
    ]
    grad_actives = [
        jnp.einsum("td,fd->tf", back, weight_d, preferred_element_type=F32).astype(LOW)
        for back in upstream
    ]
    inputs_own = chip.ring(normed2)

    def both_cores(part, *waits):
        part = hold(part, *waits)
        return core.ordered([part, core.shift(part)], 0).reshape(2 * tokens, D)

    def half_of(part, side):
        return lax.dynamic_slice_in_dim(part, (core.place + side) % 2 * tokens, tokens, 0)

    def core_sum(part):
        return half_of(part, 0) + core.shift(half_of(part, 1).astype(LOW)).astype(F32)

    inputs, actives, grad_gates, grad_upwards, grads, kept, grad_sums, outs = ([] for _ in range(8))
    for step, fed in enumerate(inputs_own):
        fed = both_cores(fed, *actives[-1:])
        inputs.append(fed)
        grad_active = grad_actives[step].astype(F32)
        gate = jnp.dot(fed, weight_g, preferred_element_type=F32)
        upward = jnp.dot(fed, weight_u, preferred_element_type=F32)
        sigmoid_gate = jax.nn.sigmoid(gate)
        active = (gate * sigmoid_gate * upward).astype(LOW)
        grad_gate = (
            grad_active * upward * sigmoid_gate * (1.0 + gate * (1.0 - sigmoid_gate))
        ).astype(LOW)
        grad_upward = (grad_active * gate * sigmoid_gate).astype(LOW)
        back_gate, back_upward = grad_gate, grad_upward
        if step == 1:
            back_gate = hold(grad_gate, grads[0])
        if step > 1:
            arrived = chip.shift(grad_sums[-1].astype(LOW))
            back_gate, back_upward = hold(grad_gate, arrived), hold(grad_upward, arrived)
        grads.append(
            jnp.einsum("tf,df->td", back_gate, weight_g, preferred_element_type=F32)
            + jnp.einsum("tf,df->td", back_upward, weight_u, preferred_element_type=F32)
        )
        kept.append(core_sum(grads[-1]))
        if step > 0:
            grad_sums.append(kept[-1] if step == 1 else arrived.astype(F32) + kept[-1])
        actives.append(active)
        outs.append(jnp.dot(active, weight_d, preferred_element_type=F32).astype(LOW))
        grad_gates.append(grad_gate)
        grad_upwards.append(grad_upward)
    arrived = chip.shift(grad_sums[-1].astype(LOW)).astype(F32)
    grad_normed2 = (arrived + kept[0]).astype(LOW)

    fed_all = jnp.concatenate(inputs, axis=0)
    def plane_sum(parts, wait):
        part = jnp.einsum(
            "td,tf->df",
            fed_all,
            hold(jnp.concatenate(parts, axis=0), wait),
            preferred_element_type=F32,
        ).astype(LOW)
        total = lax.psum_scatter(part, "ctx", scatter_dimension=0, tiled=True)
        return part, total.reshape(n_dp, rows, width)

    part_gate, sum_gate = plane_sum(grad_gates, grad_sums[-1])

    others = core.shift(jnp.stack([half_of(part, 1) for part in outs]))
    out_parts = [
        half_of(part, 0).astype(F32) + others[step].astype(F32) for step, part in enumerate(outs)
    ]
    grad_normed2 = hold(grad_normed2, part_gate, *out_parts[1:2])
    grad_normed2 = jnp.einsum("te,de->td", grad_normed2, order, preferred_element_type=F32)
    grad_gain_f, grad_middle = norm_back(grad_normed2, middle, inverse2, gain_f)
    grad_middle = grad_middle + cotangent.astype(F32)
    grad_attention = grad_middle.astype(LOW)
    grad_mixed = jnp.einsum(
        "te,de->td", grad_attention, weight_o, preferred_element_type=F32
    ).astype(LOW)
    out_sums = [hold(out_parts[1 % len(outs)], grad_attention).astype(LOW)]
    out_first = chip.shift(out_sums[0]).astype(F32)
    grad_query_rot, both_part = attend_back(
        query_rot.reshape(tokens, D), grad_mixed, both_all, bias_turned
    )
    out_sums.append(out_first + out_parts[2 % len(outs)])
    part_output = jnp.einsum(
        "td,te->de", mixed_low, hold(grad_attention, both_part), preferred_element_type=F32
    ).astype(LOW)
    core_output = core_sums(part_output)
    both_part = hold(both_part, out_first).reshape(2, n_ctx, tokens, kv_width)
    both_sum = row.direct(both_part, 1)
    grad_key_rot = both_sum[0]
    grad_values = both_sum[1].astype(LOW)
    part_up, sum_up = plane_sum(grad_upwards, both_part)
    sums = jnp.stack([sum_gate, sum_up], axis=1)
    part_down = jnp.einsum(
        "tf,td->fd",
        hold(jnp.concatenate(actives, axis=0), both_sum),
        jnp.concatenate(upstream, axis=0),
        preferred_element_type=F32,
    ).astype(LOW)[:real]
    part_down = lax.psum_scatter(part_down, "ctx", scatter_dimension=0, tiled=True)
    sums = lax.all_to_all(hold(sums, both_part), "dp", 0, 0, tiled=True)
    gate_weight_grad = sums[:, 0, :, :real].transpose(1, 0, 2).reshape(rows, -1).astype(F32)
    up_weight_grad = sums[:, 1, :, :real].transpose(1, 0, 2).reshape(rows, -1).astype(F32)
    grad_keys = (
        unturn(grad_key_rot.reshape(tokens, KV_HEADS, HEAD), cosine, sine)
        .reshape(tokens, kv_width)
        .astype(LOW)
    )
    grad_queries = (
        unturn(grad_query_rot.reshape(tokens, HEADS, HEAD), cosine, sine)
        .reshape(tokens, D)
        .astype(LOW)
    )
    joined = jnp.concatenate([grad_queries, grad_keys, grad_values], axis=1)
    out_second = chip.shift(hold(out_sums[1].astype(LOW), both_part)).astype(F32)
    joined = hold(joined, out_second)
    grad_normed = jnp.einsum(
        "te,de->td", joined[:, :half], weight_qk, preferred_element_type=F32
    ) + jnp.einsum("te,de->td", grad_values, weight_v, preferred_element_type=F32)
    grad_gain_a, grad_hidden = norm_back(grad_normed, hidden, inverse, gain_a)
    input_grad = grad_middle + grad_hidden
    part_in = jnp.einsum("td,te->de", normed, joined, preferred_element_type=F32).astype(LOW)
    bias_sums = jnp.sum(joined.astype(F32), axis=0)
    short = [
        jnp.pad(part.reshape(-1, few), ((0, 0), (0, rows - few))).reshape(D)
        for part in (bias_sums[D : D + kv_width], bias_sums[D + kv_width :])
    ]
    tile = jnp.stack([grad_gain_a, grad_gain_f, bias_sums[:D]] + short, axis=1).astype(LOW)
    tile = jnp.pad(tile, ((0, 0), (0, HEAD - tile.shape[1])))
    part_in = jnp.concatenate([part_in, tile], axis=1)
    out_sums.append(out_second + out_parts[3 % len(outs)])
    core_grads = core_sums(part_in)
    for step in range(4, n_dp // 2 + 1):
        sent = hold(out_sums[-1].astype(LOW), part_in)
        out_sums.append(chip.shift(sent).astype(F32) + out_parts[step % len(outs)])
    first_output = (
        inner.scatter(core_output[..., : D // 2], 2).astype(LOW),
        outer.scatter(core_output[..., D // 2 :], 1).astype(LOW),
    )
    plane_output = [
        outer.scatter(first_output[0], 1).astype(LOW),
        inner.scatter(first_output[1], 1).astype(LOW),
    ]
    middle_cut = mixed_width // 2
    first_grads = (
        inner.scatter(core_grads[..., :middle_cut], 2).astype(LOW),
        outer.scatter(core_grads[..., middle_cut:], 1).astype(LOW),
    )
    plane_grads = [
        outer.scatter(hold(first_grads[0], sums), 1).astype(LOW),
        inner.scatter(hold(first_grads[1], sums), 1).astype(LOW),
    ]
    plane_grads = jnp.concatenate(plane_grads + plane_output, axis=-1)
    layer_output = (middle + out_sums[-1]).astype(LOW)
    down_weight_grad = part_down.astype(F32)
    in_grads = chip.scatter(hold(plane_grads, out_sums[-1]), 0)
    output_weight_grad = in_grads[:, mixed_width + HEAD :]
    small = in_grads[:, mixed_width : mixed_width + HEAD].T
    return (
        layer_output,
        input_grad,
        small[0],
        in_grads[:, :D],
        in_grads[:, D : D + kv_width],
        in_grads[:, D + kv_width : mixed_width],
        small[2],
        small[3, :few],
        small[4, :few],
        output_weight_grad,
        small[1],
        gate_weight_grad,
        up_weight_grad,
        down_weight_grad,
    )


def solution(mesh):
    split = P(("dp", "ctx"), None)
    vector = P(("dp", "ctx"))
    placed = (
        split,
        split,
        P("dp", None),
        vector,
        split,
        split,
        split,
        vector,
        vector,
        vector,
        split,
        vector,
        split,
        split,
        split,
    )
    results = (
        split,
        split,
        vector,
        split,
        split,
        split,
        vector,
        vector,
        vector,
        split,
        vector,
        split,
        split,
        split,
    )
    return jax.shard_map(
        per_device, mesh=mesh, in_specs=placed, out_specs=results, check_vma=False
    )
```

```python
import jax
import jax.numpy as jnp
from jax import lax
from jax.experimental import pallas as pl
from jax.experimental.pallas import tpu as pltpu
from jax.sharding import PartitionSpec as P

D = 1536
HEADS = 12
KV_HEADS = 2
HEAD = 128
DOCS = 5


EPS = 1e-06
F32 = jnp.float32
LOW = jnp.bfloat16
GROUP = HEADS // KV_HEADS
VMEM_BYTES = 32 * 2**20
LAST = (((1,), (1,)), ((), ()))
FIRST = (((0,), (0,)), ((), ()))


def turn(values, cosine, sine):
    half = values.shape[-1] // 2
    first = values[..., :half]
    second = values[..., half:]
    cosine = cosine[:, None, :]
    sine = sine[:, None, :]
    return jnp.concatenate(
        [first * cosine - second * sine, second * cosine + first * sine], axis=-1
    )


def unturn(grads, cosine, sine):
    half = grads.shape[-1] // 2
    first = grads[..., :half]
    second = grads[..., half:]
    cosine = cosine[:, None, :]
    sine = sine[:, None, :]
    return jnp.concatenate(
        [first * cosine + second * sine, second * cosine - first * sine], axis=-1
    )


def product(left, right, contract):
    return lax.dot_general(left, right, contract, preferred_element_type=F32)


def attend_kernel(q_ref, k_ref, v_ref, bias_ref, o_ref):
    scores = product(q_ref[...], k_ref[...], LAST) * HEAD ** (-0.5) + bias_ref[...]
    weights = jnp.exp(scores - jnp.max(scores, axis=1, keepdims=True))
    probs = weights * (1.0 / jnp.sum(weights, axis=1, keepdims=True))
    o_ref[...] = jnp.dot(probs.astype(LOW), v_ref[...], preferred_element_type=F32).astype(LOW)


def attend(query_rot, both_all, bias):
    tokens, whole = bias.shape
    return pl.pallas_call(
        attend_kernel,
        grid=(HEADS,),
        in_specs=[
            pl.BlockSpec((tokens, HEAD), lambda h: (0, h)),
            pl.BlockSpec((whole, HEAD), lambda h: (0, h // GROUP)),
            pl.BlockSpec((whole, HEAD), lambda h: (0, KV_HEADS + h // GROUP)),
            pl.BlockSpec((tokens, whole), lambda h: (0, 0)),
        ],
        out_specs=pl.BlockSpec((tokens, HEAD), lambda h: (0, h)),
        out_shape=jax.ShapeDtypeStruct(query_rot.shape, LOW),
        compiler_params=pltpu.CompilerParams(vmem_limit_bytes=VMEM_BYTES),
        cost_estimate=pl.CostEstimate(flops=10**10, bytes_accessed=10**6, transcendentals=0),
    )(query_rot, both_all, both_all, bias)


def attend_back_kernel(q_ref, g_ref, k_ref, v_ref, bias_ref, dq_ref, dkv_ref, dk_sum, dv_sum):
    step = pl.program_id(0) % GROUP
    query, grad, key = q_ref[...], g_ref[...], k_ref[...]
    scores = product(key, query, LAST) * HEAD ** (-0.5) + bias_ref[...]
    weights = jnp.exp(scores - jnp.max(scores, axis=0, keepdims=True))
    probs = weights * (1.0 / jnp.sum(weights, axis=0, keepdims=True))
    grad_probs = product(v_ref[...], grad, LAST)
    mean = jnp.sum(probs * grad_probs, axis=0, keepdims=True)
    grad_scores = (probs * (grad_probs - mean)).astype(LOW)
    dq_ref[...] = product(grad_scores, key, FIRST) * HEAD ** (-0.5)
    dv = jnp.dot(probs.astype(LOW), grad, preferred_element_type=F32)
    dk = jnp.dot(grad_scores, query, preferred_element_type=F32)

    @pl.when(step == 0)
    def _():
        dv_sum[...] = dv
        dk_sum[...] = dk

    @pl.when(step > 0)
    def _():
        dv_sum[...] += dv
        dk_sum[...] += dk

    @pl.when(step == GROUP - 1)
    def _():
        dkv_ref[0] = (dk_sum[...] * HEAD ** (-0.5)).astype(LOW)
        dkv_ref[1] = dv_sum[...].astype(LOW)


def attend_back(query_rot, grad_mixed, both_all, bias):
    whole, tokens = bias.shape
    return pl.pallas_call(
        attend_back_kernel,
        grid=(HEADS,),
        in_specs=[
            pl.BlockSpec((tokens, HEAD), lambda h: (0, h)),
            pl.BlockSpec((tokens, HEAD), lambda h: (0, h)),
            pl.BlockSpec((whole, HEAD), lambda h: (0, h // GROUP)),
            pl.BlockSpec((whole, HEAD), lambda h: (0, KV_HEADS + h // GROUP)),
            pl.BlockSpec((whole, tokens), lambda h: (0, 0)),
        ],
        out_specs=[
            pl.BlockSpec((tokens, HEAD), lambda h: (0, h)),
            pl.BlockSpec((2, whole, HEAD), lambda h: (0, 0, h // GROUP)),
        ],
        out_shape=[
            jax.ShapeDtypeStruct(query_rot.shape, F32),
            jax.ShapeDtypeStruct((2, whole, KV_HEADS * HEAD), LOW),
        ],
        scratch_shapes=[pltpu.VMEM((whole, HEAD), F32), pltpu.VMEM((whole, HEAD), F32)],
        compiler_params=pltpu.CompilerParams(vmem_limit_bytes=VMEM_BYTES),
        cost_estimate=pl.CostEstimate(flops=2 * 10**10, bytes_accessed=10**6, transcendentals=0),
    )(query_rot, grad_mixed, both_all, both_all, bias)


def norm_back(grad_normed, hidden, inverse, gain):
    scaled = grad_normed * gain
    grad_gain = jnp.sum(grad_normed * hidden * inverse, axis=0)
    grad_hidden = inverse * scaled - hidden * inverse**3 * jnp.mean(
        scaled * hidden, axis=1, keepdims=True
    )
    return (grad_gain, grad_hidden)


def hold(value, *others):
    for other in others:
        first = other[(0,) * other.ndim]
        value = jnp.where(first != first, jnp.zeros_like(value), value)
    return value


class Line:
    def __init__(self, axis, size, stride):
        self.axis, self.size, self.stride = axis, size, stride
        total = lax.axis_size(axis)
        self.place = (lax.axis_index(axis) // stride) % size
        self.up = []
        for i in range(total):
            place = (i // stride) % size
            self.up.append((i, i + ((place + 1) % size - place) * stride))

    def shift(self, value):
        return lax.ppermute(value, self.axis, self.up)

    def ring(self, value):
        parts = [value]
        for _ in range(self.size - 1):
            parts.append(self.shift(parts[-1]))
        return parts

    def ordered(self, parts, dim):
        if self.size == 2:
            first = self.place == 0
            return jnp.stack(
                [jnp.where(first, parts[0], parts[1]), jnp.where(first, parts[1], parts[0])], dim
            )
        shape = parts[0].shape
        whole = jnp.zeros(shape[:dim] + (self.size,) + shape[dim:], parts[0].dtype)
        for step, part in enumerate(parts):
            whole = lax.dynamic_update_slice_in_dim(
                whole, jnp.expand_dims(part, dim), (self.place - step) % self.size, dim
            )
        return whole

    def gather(self, value, dim):
        return self.ordered(self.ring(value), dim)

    def direct(self, blocks, dim, *waits):
        total = self.pick(blocks, dim, 0).astype(F32)
        sent = [hold(self.pick(blocks, dim, -step), *waits) for step in range(1, self.size)]
        for step, block in enumerate(sent, 1):
            total = total + lax.ppermute(
                block, self.axis, [(i, self.there(i, step)) for i in range(len(self.up))]
            ).astype(F32)
        return total

    def there(self, i, step):
        place = (i // self.stride) % self.size
        return i + ((place + step) % self.size - place) * self.stride

    def pick(self, blocks, dim, step):
        return lax.dynamic_index_in_dim(blocks, (self.place - step) % self.size, dim, False)

    def scatter(self, blocks, dim, kind=LOW):
        total = self.pick(blocks, dim, 1)
        for step in range(2, self.size + 1):
            total = self.shift(total.astype(kind)).astype(F32)
            total = total + self.pick(blocks, dim, step).astype(F32)
        return total


def per_device(
    layer_input,
    cotangent,
    doc_lengths,
    attention_gain,
    query_weight,
    key_weight,
    value_weight,
    query_bias,
    key_bias,
    value_bias,
    output_weight,
    feedforward_gain,
    gate_weight,
    up_weight,
    down_weight,
):
    tokens = layer_input.shape[0]
    n_dp = lax.axis_size("dp")
    n_ctx = lax.axis_size("ctx")
    here = lax.axis_index("dp")
    which = lax.axis_index("ctx")
    chip = Line("dp", n_dp // 2, 2)
    core = Line("dp", 2, 1)
    outer = Line("ctx", n_ctx // 2, 2)
    inner = Line("ctx", 2, 1)
    row = Line("ctx", n_ctx, 1)
    rows = query_weight.shape[0]
    kv_width = KV_HEADS * HEAD

    def plane_gather(value, first, dim):
        if first:
            return outer.gather(inner.gather(value, dim), dim)
        return inner.gather(outer.gather(value, dim), dim + 1)

    def plane_scatter(blocks, first, dim, kind=LOW):
        if first:
            return outer.scatter(inner.scatter(blocks, dim + 1, kind), dim, kind)
        return inner.scatter(outer.scatter(blocks, dim, kind), dim, kind)

    def plane_gather_halves(value, cut, dim):
        first = (inner.gather(value[..., :cut], dim), outer.gather(value[..., cut:], dim))
        first = (hold(first[0], first[1]), hold(first[1], first[0]))
        return (outer.gather(first[0], dim), inner.gather(first[1], dim + 1))

    def core_sums(array):
        blocks = array.reshape((n_dp // 2, 2, n_ctx // 2, 2, rows) + array.shape[1:])
        return core.scatter(blocks, 1).astype(LOW)

    few = key_bias.shape[0]
    tile = jnp.stack(
        [attention_gain, feedforward_gain, query_bias]
        + [jnp.pad(part, (0, rows - few)) for part in (key_bias, value_bias)],
        axis=1,
    )
    tile = jnp.pad(tile, ((0, 0), (0, HEAD - tile.shape[1])))
    mixed_width = D + 2 * kv_width
    half = D + kv_width
    ring_in = chip.ring(
        jnp.concatenate([query_weight, key_weight, value_weight, output_weight, tile], axis=1)
    )
    cut = D // 2
    down_first = (inner.gather(down_weight[:, :cut], 0), outer.gather(down_weight[:, cut:], 0))
    plane_in = plane_gather_halves(hold(chip.ordered(ring_in, 0), *down_first), half, 1)
    upstream_all = lax.all_gather(hold(cotangent, ring_in[-1]), "dp", axis=0, tiled=True)

    real = gate_weight.shape[1] // n_dp
    width = -(-real // HEAD) * HEAD
    units = jnp.stack(
        [gate_weight.reshape(rows, n_dp, real), up_weight.reshape(rows, n_dp, real)]
    ).transpose(2, 0, 1, 3)
    units = jnp.pad(units, ((0, 0), (0, 0), (0, 0), (0, width - real)))
    units = lax.all_to_all(hold(units, *plane_in), "dp", 0, 0, tiled=True)
    weight_qk, weight_rest = [core.gather(hold(part, *plane_in), 1).reshape(D, -1) for part in plane_in]
    weight_v = weight_rest[:, :kv_width]
    weight_o = weight_rest[:, kv_width : kv_width + D]
    vectors = weight_rest[:, kv_width + D :].astype(F32).T
    gain_a, gain_f, bias_q = vectors[0], vectors[1], vectors[2]
    bias_k, bias_v = (
        vectors[i].reshape(-1, rows)[:, :few].reshape(-1) for i in (3, 4)
    )

    place = jnp.arange(D, dtype=jnp.int32)
    source = ((place // rows) % n_dp * n_ctx + place // (rows * n_dp)) * rows + place % rows
    order = (place[:, None] == source[None, :]).astype(LOW)

    whole = tokens * n_ctx
    places = jnp.arange(whole, dtype=jnp.int32)
    lengths = doc_lengths[0]
    entry = jnp.arange(DOCS, dtype=jnp.int32)
    ends = jnp.sum(jnp.where(entry[None, :] <= entry[:, None], lengths[None, :], 0), axis=1)
    starts = ends - lengths
    segment = jnp.sum((places[:, None] >= ends[None, :]).astype(jnp.int32), axis=1)
    chosen = (segment[:, None] == entry[None, :]).astype(jnp.int32)
    offsets = places - jnp.sum(chosen * starts[None, :], axis=1)
    padded = segment == DOCS - 1
    first_row = which * tokens
    mine = lax.dynamic_slice_in_dim(places, first_row, tokens)
    my_segment = lax.dynamic_slice_in_dim(segment, first_row, tokens)
    my_offsets = lax.dynamic_slice_in_dim(offsets, first_row, tokens)
    allowed = (places[None, :] <= mine[:, None]) & (segment[None, :] == my_segment[:, None])
    allowed = allowed & (jnp.logical_not(padded)[None, :] | (places[None, :] == mine[:, None]))
    bias = jnp.where(allowed, 0.0, -1e30).astype(F32)
    turned = (places[:, None] <= mine[None, :]) & (segment[:, None] == my_segment[None, :])
    turned = turned & (jnp.logical_not(padded)[:, None] | (places[:, None] == mine[None, :]))
    bias_turned = jnp.where(turned, 0.0, -1e30).astype(F32)
    freqs = 10000.0 ** (-jnp.arange(0, HEAD // 2, dtype=F32) * 2.0 / HEAD)
    angles = my_offsets.astype(F32)[:, None] * freqs[None, :]
    cosine = jnp.cos(angles)
    sine = jnp.sin(angles)

    hidden = layer_input.astype(F32)
    inverse = lax.rsqrt(jnp.mean(hidden * hidden, axis=1, keepdims=True) + EPS)
    normed = (hidden * inverse * gain_a).astype(LOW)
    projected = jnp.dot(normed, weight_qk, preferred_element_type=F32)
    queries = projected[:, :D] + bias_q
    keys = projected[:, D:] + bias_k
    values = jnp.dot(normed, weight_v, preferred_element_type=F32) + bias_v
    query_rot = turn(queries.reshape(tokens, HEADS, HEAD), cosine, sine).astype(LOW)
    key_rot = (
        turn(keys.reshape(tokens, KV_HEADS, HEAD), cosine, sine)
        .astype(LOW)
        .reshape(tokens, kv_width)
    )
    value_low = values.astype(LOW)
    down_parts = (
        outer.gather(hold(down_first[0], weight_qk), 0),
        inner.gather(hold(down_first[1], weight_qk), 1),
    )
    weight_d = jnp.concatenate([part.reshape(real, cut) for part in down_parts], axis=1)
    weight_d = jnp.pad(weight_d, ((0, width - real), (0, 0)))
    both = hold(jnp.concatenate([key_rot, value_low], axis=1), *down_parts)
    both_all = jnp.zeros((n_ctx,) + both.shape, LOW)
    for step in range(n_ctx):
        arrived = both
        if step:
            arrived = lax.ppermute(both, "ctx", [(i, (i + step) % n_ctx) for i in range(n_ctx)])
        both_all = lax.dynamic_update_slice_in_dim(
            both_all, arrived[None], (which - step) % n_ctx, 0
        )
    both_all = both_all.reshape(whole, 2 * kv_width)
    units = units.transpose(1, 0, 2, 3).reshape(2 * n_dp * rows, width)
    units_all = lax.all_gather(hold(units, both), "ctx", axis=0, tiled=True)
    units_all = units_all.reshape(n_ctx, 2, n_dp * rows, width)
    weight_g, weight_u = (units_all[:, i].reshape(D, width) for i in (0, 1))
    mixed_low = attend(query_rot.reshape(tokens, D), both_all, bias)
    middle = hidden + jnp.dot(mixed_low, weight_o, preferred_element_type=F32)

    inverse2 = lax.rsqrt(jnp.mean(middle * middle, axis=1, keepdims=True) + EPS)
    normed2 = (middle * inverse2 * gain_f).astype(LOW)
    normed2 = jnp.dot(normed2, order, preferred_element_type=F32).astype(LOW)
    upstream = [
        lax.dynamic_slice_in_dim(
            upstream_all, (chip.place - step) % chip.size * 2 * tokens, 2 * tokens, 0
        )
        for step in range(n_dp // 2)
    ]
    grad_actives = [
        jnp.einsum("td,fd->tf", back, weight_d, preferred_element_type=F32).astype(LOW)
        for back in upstream
    ]
    inputs_own = [normed2, chip.shift(normed2)]
    for step in range(2, n_dp // 2):
        waits = grad_actives if step == 2 else ()
        inputs_own.append(chip.shift(hold(inputs_own[-1], *waits)))

    def both_cores(part, *waits):
        part = hold(part, *waits)
        return core.ordered([part, core.shift(part)], 0).reshape(2 * tokens, D)

    def half_of(part, side):
        return lax.dynamic_slice_in_dim(part, (core.place + side) % 2 * tokens, tokens, 0)

    def core_sum(part):
        return half_of(part, 0) + core.shift(half_of(part, 1).astype(LOW)).astype(F32)

    inputs, actives, grad_gates, grad_upwards, grads, kept, grad_sums, outs = ([] for _ in range(8))
    for step, fed in enumerate(inputs_own):
        fed = both_cores(fed, *actives[-1:])
        inputs.append(fed)
        grad_active = grad_actives[step].astype(F32)
        gate = jnp.dot(fed, weight_g, preferred_element_type=F32)
        upward = jnp.dot(fed, weight_u, preferred_element_type=F32)
        sigmoid_gate = jax.nn.sigmoid(gate)
        active = (gate * sigmoid_gate * upward).astype(LOW)
        grad_gate = (
            grad_active * upward * sigmoid_gate * (1.0 + gate * (1.0 - sigmoid_gate))
        ).astype(LOW)
        grad_upward = (grad_active * gate * sigmoid_gate).astype(LOW)
        back_gate = grad_gate
        if step == 1:
            back_gate = hold(grad_gate, grads[0])
        if step > 1:
            arrived = chip.shift(grad_sums[-1].astype(LOW))
            back_gate = hold(grad_gate, arrived)
        grads.append(
            jnp.einsum("tf,df->td", back_gate, weight_g, preferred_element_type=F32)
            + jnp.einsum("tf,df->td", grad_upward, weight_u, preferred_element_type=F32)
        )
        kept.append(core_sum(grads[-1]))
        if step > 0:
            grad_sums.append(kept[-1] if step == 1 else arrived.astype(F32) + kept[-1])
        actives.append(active)
        outs.append(jnp.dot(active, weight_d, preferred_element_type=F32).astype(LOW))
        grad_gates.append(grad_gate)
        grad_upwards.append(grad_upward)
    arrived = chip.shift(grad_sums[-1].astype(LOW)).astype(F32)
    grad_normed2 = (arrived + kept[0]).astype(LOW)

    fed_all = jnp.concatenate(inputs, axis=0)
    def plane_sum(parts, wait):
        part = jnp.einsum(
            "td,tf->df",
            fed_all,
            hold(jnp.concatenate(parts, axis=0), wait),
            preferred_element_type=F32,
        ).astype(LOW)
        total = lax.psum_scatter(part, "ctx", scatter_dimension=0, tiled=True)
        return part, total.reshape(n_dp, rows, width)

    part_gate, sum_gate = plane_sum(grad_gates, grad_sums[-1])

    others = core.shift(jnp.stack([half_of(part, 1) for part in outs]))
    out_parts = [
        half_of(part, 0).astype(F32) + others[step].astype(F32) for step, part in enumerate(outs)
    ]
    grad_normed2 = hold(grad_normed2, part_gate, *out_parts[1:2])
    grad_normed2 = jnp.einsum("te,de->td", grad_normed2, order, preferred_element_type=F32)
    grad_gain_f, grad_middle = norm_back(grad_normed2, middle, inverse2, gain_f)
    grad_middle = grad_middle + cotangent.astype(F32)
    grad_attention = grad_middle.astype(LOW)
    grad_mixed = jnp.einsum(
        "te,de->td", grad_attention, weight_o, preferred_element_type=F32
    ).astype(LOW)
    out_sums = [hold(out_parts[1 % len(outs)], grad_attention).astype(LOW)]
    out_first = chip.shift(out_sums[0]).astype(F32)
    grad_query_rot, both_part = attend_back(
        query_rot.reshape(tokens, D), grad_mixed, both_all, bias_turned
    )
    out_sums.append(out_first + out_parts[2 % len(outs)])
    part_output = jnp.einsum(
        "td,te->de", mixed_low, hold(grad_attention, both_part), preferred_element_type=F32
    ).astype(LOW)
    core_output = core_sums(part_output)
    both_part = hold(both_part, out_first).reshape(2, n_ctx, tokens, kv_width)
    both_sum = row.direct(both_part, 1)
    grad_key_rot = both_sum[0]
    grad_values = both_sum[1].astype(LOW)
    part_up, sum_up = plane_sum(grad_upwards, both_part)
    sums = jnp.stack([sum_gate, sum_up], axis=1)
    part_down = jnp.einsum(
        "tf,td->fd",
        hold(jnp.concatenate(actives, axis=0), both_sum),
        jnp.concatenate(upstream, axis=0),
        preferred_element_type=F32,
    ).astype(LOW)[:real]
    part_down = lax.psum_scatter(part_down, "ctx", scatter_dimension=0, tiled=True)
    sums = lax.all_to_all(hold(sums, both_part), "dp", 0, 0, tiled=True)
    gate_weight_grad = sums[:, 0, :, :real].transpose(1, 0, 2).reshape(rows, -1).astype(F32)
    up_weight_grad = sums[:, 1, :, :real].transpose(1, 0, 2).reshape(rows, -1).astype(F32)
    grad_keys = (
        unturn(grad_key_rot.reshape(tokens, KV_HEADS, HEAD), cosine, sine)
        .reshape(tokens, kv_width)
        .astype(LOW)
    )
    grad_queries = (
        unturn(grad_query_rot.reshape(tokens, HEADS, HEAD), cosine, sine)
        .reshape(tokens, D)
        .astype(LOW)
    )
    joined = jnp.concatenate([grad_queries, grad_keys, grad_values], axis=1)
    out_second = chip.shift(hold(out_sums[1].astype(LOW), both_part)).astype(F32)
    joined = hold(joined, out_second)
    grad_normed = jnp.einsum(
        "te,de->td", joined[:, :half], weight_qk, preferred_element_type=F32
    ) + jnp.einsum("te,de->td", grad_values, weight_v, preferred_element_type=F32)
    grad_gain_a, grad_hidden = norm_back(grad_normed, hidden, inverse, gain_a)
    input_grad = grad_middle + grad_hidden
    part_in = jnp.einsum("td,te->de", normed, joined, preferred_element_type=F32).astype(LOW)
    bias_sums = jnp.sum(joined.astype(F32), axis=0)
    short = [
        jnp.pad(part.reshape(-1, few), ((0, 0), (0, rows - few))).reshape(D)
        for part in (bias_sums[D : D + kv_width], bias_sums[D + kv_width :])
    ]
    tile = jnp.stack([grad_gain_a, grad_gain_f, bias_sums[:D]] + short, axis=1).astype(LOW)
    tile = jnp.pad(tile, ((0, 0), (0, HEAD - tile.shape[1])))
    part_in = jnp.concatenate([part_in, tile], axis=1)
    out_sums.append(out_second + out_parts[3 % len(outs)])
    core_grads = core_sums(part_in)
    for step in range(4, n_dp // 2 + 1):
        sent = hold(out_sums[-1].astype(LOW), part_in)
        out_sums.append(chip.shift(sent).astype(F32) + out_parts[step % len(outs)])
    first_output = (
        inner.scatter(core_output[..., : D // 2], 2).astype(LOW),
        outer.scatter(core_output[..., D // 2 :], 1).astype(LOW),
    )
    plane_output = [
        outer.scatter(first_output[0], 1).astype(LOW),
        inner.scatter(first_output[1], 1).astype(LOW),
    ]
    middle_cut = mixed_width // 2
    first_grads = (
        inner.scatter(core_grads[..., :middle_cut], 2).astype(LOW),
        outer.scatter(core_grads[..., middle_cut:], 1).astype(LOW),
    )
    plane_grads = [
        outer.scatter(hold(first_grads[0], sums), 1).astype(LOW),
        inner.scatter(hold(first_grads[1], sums), 1).astype(LOW),
    ]
    plane_grads = jnp.concatenate(plane_grads + plane_output, axis=-1)
    layer_output = (middle + out_sums[-1]).astype(LOW)
    down_weight_grad = part_down.astype(F32)
    in_grads = chip.scatter(hold(plane_grads, out_sums[-1]), 0)
    output_weight_grad = in_grads[:, mixed_width + HEAD :]
    small = in_grads[:, mixed_width : mixed_width + HEAD].T
    return (
        layer_output,
        input_grad,
        small[0],
        in_grads[:, :D],
        in_grads[:, D : D + kv_width],
        in_grads[:, D + kv_width : mixed_width],
        small[2],
        small[3, :few],
        small[4, :few],
        output_weight_grad,
        small[1],
        gate_weight_grad,
        up_weight_grad,
        down_weight_grad,
    )


def solution(mesh):
    split = P(("dp", "ctx"), None)
    vector = P(("dp", "ctx"))
    placed = (
        split,
        split,
        P("dp", None),
        vector,
        split,
        split,
        split,
        vector,
        vector,
        vector,
        split,
        vector,
        split,
        split,
        split,
    )
    results = (
        split,
        split,
        vector,
        split,
        split,
        split,
        vector,
        vector,
        vector,
        split,
        vector,
        split,
        split,
        split,
    )
    return jax.shard_map(
        per_device, mesh=mesh, in_specs=placed, out_specs=results, check_vma=False
    )
```
